128 devices in a mesh: slab: 8 (over x, core), owner: 16 (over z, y).
Axes of the slice: x: 4, y: 4, z: 4, core: 2. Of those that a mesh axis runs over, the one named last changes fastest.
Arguments:
- observed: float32 [512, 2048, 128], P('slab', 'owner'), may hold values from 0.2 to 5
- tissue: int32 [16, 64], P('slab', 'owner'), may hold values from 0 to 1, as said below
- point_spread: float32 [3, 33], replicated, may hold values from 0.05 to 1
Outputs:
- packed: float32 [896, 32, 32, 128], P(('slab', 'owner'))
The draws below stay inside these ranges and needn't reach their ends.
Inputs may be any that keep to these rules, and one draw needn't show every extreme that they name: Every row group of 2 tile rows holds exactly 112 tissue tiles; within a row group, the 2 x 4 block of tiles with column block index c (columns c * 4 to (c + 1) * 4 - 1) holds all its tiles as tissue for even c and 6 of them for odd c.
All inputs are finite; a program needn't handle non-finite values.
Results may differ from the reference program's by a relative error of at most 0.0001.
Values sent between devices are 32-bit elements; how exact they have to be, the bound alone decides.
No kernel may reach another device: no remote copies, remote signals or barrier semaphores. Data moves between devices by JAX's collectives and lax.ppermute only.
A program may use at most 128 MiB of HBM per device.

```python
import math
import jax
import jax.numpy as jnp
from jax import lax

TILE = 32
TX_DEV = 2
TY_DEV = 4
PLANES = 128
TAPS = 33
ITERS = 2
CAP = 7
TROWS = 16
TCOLS = 64
NX = 512
NY = 2048
PACKED = 896
N_SLAB = 8
N_OWNER = 16


def draw_tissue(key, part):
    key = jax.random.fold_in(key, 7)
    per_block = TX_DEV * TY_DEV
    kept_odd = 2 * CAP - per_block
    noise_int = jax.random.randint(key, (N_SLAB, N_OWNER, per_block), 0, 1024, dtype=jnp.int32)
    distinct = noise_int * per_block + jnp.arange(per_block, dtype=jnp.int32)[None, None, :]
    kept_floor = lax.top_k(distinct, kept_odd)[0][:, :, -1]
    odd_keep = (distinct >= kept_floor[:, :, None]).astype(jnp.int32)
    parity = (jnp.arange(N_OWNER, dtype=jnp.int32) % 2)[None, :, None]
    chosen = jnp.where(parity == 0, jnp.ones_like(odd_keep), odd_keep).astype(jnp.int32)
    chosen = chosen.reshape(N_SLAB, N_OWNER, TX_DEV, TY_DEV).transpose(0, 2, 1, 3)
    return chosen.reshape(TROWS, TCOLS)


def level_of(stream_key, shape, shards, least, high):
    level, own = 1.0, jax.random.fold_in(stream_key, 6)
    for dim, parts in shards:
        heights = jnp.exp(jax.random.uniform(jax.random.fold_in(own, dim), (parts,), jnp.float32, least / len(shards), high / len(shards)))
        level = level * jnp.repeat(heights, shape[dim] // parts).reshape([-1 if axis == dim else 1 for axis in range(len(shape))])
    return level


def setup_inputs(seed: int = 0) -> dict:
    splits = jax.random.split(jax.random.key(seed), 4)
    return {
        "observed": jnp.clip(jnp.exp(math.log(5.0) - 3.218876 * jax.random.uniform(splits[0], (NX, NY, PLANES), jnp.float32) ** level_of(splits[0], (NX, NY, PLANES), ((0, 8), (1, 16)), -0.2, 0.2)), 0.2, 5.0),
        "tissue": draw_tissue(jax.random.fold_in(splits[3], 71), 0),
        "point_spread": jnp.clip(jnp.exp(jax.random.uniform(splits[2], (3, TAPS), jnp.float32, math.log(0.05), math.log(1.0))), 0.05, 1.0),
    }


ratio_floor = 0.05


def correlate(values, weights, axis_index):
    half_span = (weights.shape[0] - 1) // 2
    widths = [(0, 0)] * values.ndim
    widths[axis_index] = (half_span, half_span)
    padded = jnp.pad(values, widths)
    length = values.shape[axis_index]
    summed = jnp.zeros_like(values)
    for position in range(weights.shape[0]):
        summed = summed + weights[position] * lax.slice_in_dim(padded, position, position + length, axis=axis_index)
    return summed


def spread(values, normed):
    partial_value = correlate(values, normed[0], 0)
    partial_value = correlate(partial_value, normed[1], 1)
    return correlate(partial_value, normed[2], 2)


def reference(observed, tissue, point_spread):
    normed = point_spread / jnp.sum(point_spread, axis=1, keepdims=True)
    flipped = normed[:, ::-1]
    voxel_mask = jnp.repeat(jnp.repeat(tissue, TILE, axis=0), TILE, axis=1).astype(observed.dtype)
    masked = observed * voxel_mask[:, :, None]
    estimate = masked
    for iteration in range(ITERS):
        blurred = spread(estimate, normed)
        ratio_field = masked / jnp.maximum(blurred, ratio_floor)
        estimate = estimate * spread(ratio_field, flipped)
    blocks = estimate.reshape(N_SLAB, TX_DEV, TILE, N_OWNER, TY_DEV, TILE, PLANES)
    blocks = blocks.transpose(0, 3, 1, 4, 2, 5, 6).reshape(N_SLAB, N_OWNER * TX_DEV * TY_DEV, TILE, TILE, PLANES)
    tile_flags = tissue.reshape(N_SLAB, TX_DEV, N_OWNER, TY_DEV).transpose(0, 2, 1, 3)
    tile_flags = tile_flags.reshape(N_SLAB, N_OWNER * TX_DEV * TY_DEV).astype(jnp.int32)
    tile_rank = jnp.cumsum(tile_flags, axis=1).astype(jnp.int32) - tile_flags
    target = (tile_rank % N_OWNER) * CAP + tile_rank // N_OWNER
    target = jnp.where(tile_flags > 0, target, N_OWNER * CAP).astype(jnp.int32)
    group_index = jnp.broadcast_to(jnp.arange(N_SLAB, dtype=jnp.int32)[:, None], target.shape)
    packed = jnp.zeros((N_SLAB, N_OWNER * CAP, TILE, TILE, PLANES), estimate.dtype)
    packed = packed.at[group_index, target].set(blocks, mode="drop")
    return packed.reshape(PACKED, TILE, TILE, PLANES)
```

```python
import jax
import jax.numpy as jnp
from jax import lax
from jax.experimental import pallas as pl
from jax.experimental.pallas import tpu as pltpu
from jax.sharding import PartitionSpec as P

ITERS = 2
ratio_floor = 0.05

BX, BY, BZ = 64, 128, 128
TAPS, HALF = 33, 16
EDGE = 32
TILES = 8
CAP = 7
OWNERS = 16
GROUPS = BX // 16
OCT = BY // 8
WIDE = 8

bf16 = jnp.bfloat16
f32 = jnp.float32
VM = pl.BlockSpec(memory_space=pltpu.VMEM)
SM = pl.BlockSpec(memory_space=pltpu.SMEM)
PARAMS = pltpu.CompilerParams(vmem_limit_bytes=26 << 20)


def first_rank(c):
    return 7 * c if c % 2 == 0 else 7 * (c - 1) + 8


def tile_edges():
    out = []
    for c in range(OWNERS):
        for k in range(8 if c % 2 == 0 else 6):
            rank = first_rank(c) + k
            out.append((c, rank % OWNERS, k, rank // OWNERS))
    return out


def matching(edges, must_src, must_dst):
    adj = {}
    for e in edges:
        adj.setdefault(e[0], []).append(e)
    best = {}

    def solve(src_list, by_dst):
        def augment(s, seen):
            for e in adj.get(s, []):
                if e[1] in seen:
                    continue
                seen.add(e[1])
                if e[1] not in by_dst or augment(by_dst[e[1]][0], seen):
                    by_dst[e[1]] = e
                    return True
            return False

        for s in src_list:
            augment(s, set())
        return by_dst

    best = solve(sorted(adj, key=lambda s: (s not in must_src, s)), {})
    return sorted(best.values())


def colour(edges):
    colours = max(
        max(sum(e[0] == v for e in edges), sum(e[1] == v for e in edges)) for v in range(OWNERS)
    )
    at_src = [[None] * colours for _ in range(OWNERS)]
    at_dst = [[None] * colours for _ in range(OWNERS)]
    for e in edges:
        s, d = e[0], e[1]
        a = at_src[s].index(None)
        b = at_dst[d].index(None)
        if a != b and at_dst[d][a] is not None:
            path, side, v, c = [], "d", d, a
            while True:
                nxt = (at_dst if side == "d" else at_src)[v][c]
                if nxt is None:
                    break
                path.append((nxt, c))
                v = nxt[0] if side == "d" else nxt[1]
                side = "s" if side == "d" else "d"
                c = b if c == a else a
            for edge, c in path:
                at_src[edge[0]][c] = None
                at_dst[edge[1]][c] = None
            for edge, c in path:
                n = b if c == a else a
                at_src[edge[0]][n] = edge
                at_dst[edge[1]][n] = edge
        at_src[s][a] = e
        at_dst[d][a] = e
    return [[at_src[s][c] for s in range(OWNERS) if at_src[s][c] is not None] for c in range(colours)]


EDGES = tile_edges()
SENDS = colour([e for e in EDGES if e[0] != e[1]])
NSEND = len(SENDS)
GIVES = [[0] * (NSEND + 1) for _ in range(OWNERS)]
TAKES = [[-1] * (NSEND + 1) for _ in range(OWNERS)]
for _c, _step in enumerate(SENDS + [[e for e in EDGES if e[0] == e[1]]]):
    for _e in _step:
        GIVES[_e[0]][_c] = _e[2]
        TAKES[_e[1]][_c] = _e[3]


def parts(values):
    high = values.astype(bf16)
    return high, (values - high.astype(f32)).astype(bf16)


def weight_kernel(taps_ref, rows_ref, x_ref, y_ref, z_ref):
    total = jnp.sum(rows_ref[...], axis=1, keepdims=True)

    def band(axis, distance, flip):
        acc = jnp.zeros(distance.shape, f32)
        for k in range(TAPS):
            tap = taps_ref[axis, TAPS - 1 - k if flip else k]
            acc = jnp.where(distance == k, tap, acc)
        return acc / total[axis : axis + 1, :]

    def grid(rows, cols):
        return (
            lax.broadcasted_iota(jnp.int32, (rows, cols), 0),
            lax.broadcasted_iota(jnp.int32, (rows, cols), 1),
        )

    for flip in (0, 1):
        r, c = grid(128, 384)
        inside = (r % 8) == (c % 8)
        high, low = parts(band(0, jnp.where(inside, c // 8 - r // 8, -1), flip))
        x_ref[flip, :, 0:384] = high
        x_ref[flip, :, 384:768] = high
        x_ref[flip, :, 768:1152] = low
        r, c = grid(BY, BY + 2 * HALF)
        high, low = parts(band(1, c - r, flip))
        y_ref[flip] = jnp.concatenate([high, high, low], axis=1)
        r, c = grid(BZ, BZ)
        high, low = parts(band(2, r - c + HALF, flip))
        z_ref[flip, 0:128, 0:128] = high
        z_ref[flip, 128:256, 0:128] = high
        z_ref[flip, 0:128, 128:256] = low
        z_ref[flip, 128:256, 128:256] = jnp.zeros((128, 128), bf16)


def make_weights(point_spread):
    return pl.pallas_call(
        weight_kernel,
        out_shape=(
            jax.ShapeDtypeStruct((2, 128, 1152), bf16),
            jax.ShapeDtypeStruct((2, 128, 480), bf16),
            jax.ShapeDtypeStruct((2, 256, 256), bf16),
        ),
        in_specs=[SM, VM],
        out_specs=(VM, VM, VM),
        compiler_params=PARAMS,
        name="weights",
    )(point_spread, point_spread)


def z_pass(rows, weights):
    high, low = parts(rows)
    both = jnp.dot(
        jnp.concatenate([high, low], axis=1), weights, preferred_element_type=f32
    )
    return both[:, :128] + both[:, 128:]


def y_rows(lines, weights, row0, high_ref, low_ref):
    high, low = parts(jnp.concatenate(lines, axis=1))
    out = jnp.dot(weights, jnp.concatenate([high, low, high], axis=0), preferred_element_type=f32)
    out = jnp.concatenate(
        [out[:, 128 * i : 128 * i + 128].reshape(OCT, 8, 128) for i in range(len(lines))], axis=1
    )
    high, low = parts(out)
    rows = pl.ds(pl.multiple_of(row0 * 8, 64), 8 * len(lines))
    high_ref[:, rows, :] = high
    low_ref[:, rows, :] = low


def y_phase(own, halos, y_ref, flip, high_ref, low_ref):
    xm, xp, ym, yp, cm, cp = halos
    weights = y_ref[flip]

    def own_step(i, carry):
        x0 = i * 8
        lines = [
            jnp.concatenate([ym[x0 + k], own[x0 + k], yp[x0 + k]], axis=0) for k in range(8)
        ]
        y_rows(lines, weights, x0 + HALF, high_ref, low_ref)
        return carry

    lax.fori_loop(0, BX // 8, own_step, 0)
    for halo, corner, start in ((xm, cm, 0), (xp, cp, BX + HALF)):

        def halo_step(i, carry, halo=halo, corner=corner, start=start):
            x0 = i * 8
            lines = [
                jnp.concatenate(
                    [corner[x0 + k, :HALF], halo[x0 + k], corner[x0 + k, HALF:]], axis=0
                )
                for k in range(8)
            ]
            y_rows(lines, weights, x0 + start, high_ref, low_ref)
            return carry

        lax.fori_loop(0, HALF // 8, halo_step, 0)


def x_phase(x_ref, flip, high_ref, low_ref, finish):
    weights = x_ref[flip]

    def step(q, carry):
        o0 = q * WIDE
        for g in range(GROUPS):
            rows = slice(128 * g, 128 * g + 384)
            high = jnp.concatenate([high_ref[o0 + i, rows] for i in range(WIDE)], axis=1)
            low = jnp.concatenate([low_ref[o0 + i, rows] for i in range(WIDE)], axis=1)
            out = jnp.dot(
                weights, jnp.concatenate([high, low, high], axis=0), preferred_element_type=f32
            )
            finish(g, o0, [out[:, 128 * i : 128 * i + 128] for i in range(WIDE)])
        return carry

    lax.fori_loop(0, OCT // WIDE, step, 0)


def get(ref, g, o):
    piece = ref[16 * g : 16 * g + 16, pl.ds(pl.multiple_of(o * 8, 8), 8), :]
    return piece.reshape(128, 128)


def put(ref, g, o, piece):
    ref[16 * g : 16 * g + 16, pl.ds(pl.multiple_of(o * 8, 8), 8), :] = piece.reshape(16, 8, 128)


def masked_piece(observed, tissue, g, o):
    return get(observed, g, o) * tissue[g // 2, o // 4].astype(f32)


def strips(out, xs_lo, xs_hi, ys_lo, ys_hi):
    ys_lo[...] = out[:, :HALF, :]
    ys_hi[...] = out[:, BY - HALF :, :]
    xs_lo[...] = out[:HALF]
    xs_hi[...] = out[BX - HALF :]


STRIPS = (
    jax.ShapeDtypeStruct((HALF, BY, BZ), f32),
    jax.ShapeDtypeStruct((HALF, BY, BZ), f32),
    jax.ShapeDtypeStruct((BX, HALF, BZ), f32),
    jax.ShapeDtypeStruct((BX, HALF, BZ), f32),
)
BLOCK = jax.ShapeDtypeStruct((BX, BY, BZ), f32)
SCRATCH = [
    pltpu.VMEM((OCT, 8 * (BX + 2 * HALF), 128), bf16),
    pltpu.VMEM((OCT, 8 * (BX + 2 * HALF), 128), bf16),
]


def first_kernel(tissue, observed, z_ref, out, *edges):
    def step(q, carry):
        for g in range(GROUPS):
            pieces = [masked_piece(observed, tissue, g, q * WIDE + i) for i in range(WIDE)]
            done = z_pass(jnp.concatenate(pieces, axis=0), z_ref[0])
            for i in range(WIDE):
                put(out, g, q * WIDE + i, done[128 * i : 128 * i + 128])
        return carry

    lax.fori_loop(0, OCT // WIDE, step, 0)
    strips(out, *edges)


def first_call(tissue, observed, wz):
    return pl.pallas_call(
        first_kernel,
        out_shape=(BLOCK,) + STRIPS,
        in_specs=[SM, VM, VM],
        out_specs=(VM,) * 5,
        compiler_params=PARAMS,
        name="first",
    )(tissue, observed, wz)


def ratio_kernel(tissue, observed, own, xm, xp, ym, yp, cm, cp, x_ref, y_ref, out, *rest):
    edges, (high_ref, low_ref) = rest[:4], rest[4:]
    y_phase(own, (xm, xp, ym, yp, cm, cp), y_ref, 0, high_ref, low_ref)

    def finish(g, o0, blurred):
        for i, piece in enumerate(blurred):
            masked = masked_piece(observed, tissue, g, o0 + i)
            put(out, g, o0 + i, masked / jnp.maximum(piece, ratio_floor))

    x_phase(x_ref, 0, high_ref, low_ref, finish)
    strips(out, *edges)


def ratio_call(tissue, observed, own, halos, wx, wy):
    return pl.pallas_call(
        ratio_kernel,
        out_shape=(BLOCK,) + STRIPS,
        in_specs=[SM] + [VM] * 10,
        out_specs=(VM,) * 5,
        scratch_shapes=SCRATCH,
        compiler_params=PARAMS,
        name="ratio",
    )(tissue, observed, own, *halos, wx, wy)


def update_kernel(tissue, observed, own, xm, xp, ym, yp, cm, cp, x_ref, y_ref, z_ref, est, out, *rest):
    edges, (high_ref, low_ref) = rest[:4], rest[4:]
    y_phase(own, (xm, xp, ym, yp, cm, cp), y_ref, 1, high_ref, low_ref)

    def finish(g, o0, pieces):
        factor = z_pass(jnp.concatenate(pieces, axis=0), z_ref[1])
        old = jnp.concatenate(
            [masked_piece(observed, tissue, g, o0 + i) for i in range(WIDE)], axis=0
        )
        new = old * factor
        spread = z_pass(new, z_ref[0])
        for i in range(WIDE):
            rows = slice(128 * i, 128 * i + 128)
            put(est, g, o0 + i, new[rows])
            put(out, g, o0 + i, spread[rows])

    x_phase(x_ref, 1, high_ref, low_ref, finish)
    strips(out, *edges)


def update_call(tissue, observed, own, halos, wx, wy, wz):
    return pl.pallas_call(
        update_kernel,
        out_shape=(BLOCK, BLOCK) + STRIPS,
        in_specs=[SM] + [VM] * 11,
        out_specs=(VM,) * 6,
        scratch_shapes=SCRATCH,
        compiler_params=PARAMS,
        name="update",
    )(tissue, observed, own, *halos, wx, wy, wz)


def final_kernel(tissue, gives, est, own, xm, xp, ym, yp, cm, cp, x_ref, y_ref, z_ref, *rest):
    sends, (high_ref, low_ref, tiles, nth) = rest[: NSEND + 1], rest[NSEND + 1 :]
    y_phase(own, (xm, xp, ym, yp, cm, cp), y_ref, 1, high_ref, low_ref)
    for t in range(TILES):
        nth[t] = 0
    count = jnp.int32(0)
    for t in range(TILES):
        flag = tissue[t // 4, t % 4]

        @pl.when(flag > 0)
        def _(t=t, count=count):
            nth[count] = t

        count = count + (flag > 0).astype(jnp.int32)

    def finish(g, o0, pieces):
        factor = z_pass(jnp.concatenate(pieces, axis=0), z_ref[1])
        for i in range(WIDE):
            o = o0 + i
            new = get(est, g, o) * factor[128 * i : 128 * i + 128]
            tile = (g // 2) * 4 + o0 // 4 + i // 4
            tiles[
                tile, 16 * (g % 2) : 16 * (g % 2) + 16, 8 * (i % 4) : 8 * (i % 4) + 8, :
            ] = new.reshape(16, 8, 128)

    x_phase(x_ref, 1, high_ref, low_ref, finish)
    for c, send in enumerate(sends):
        send[...] = tiles[nth[gives[c]]]


def final_call(tissue, gives, est, own, halos, wx, wy, wz):
    tile = jax.ShapeDtypeStruct((EDGE, EDGE, BZ), f32)
    return pl.pallas_call(
        final_kernel,
        out_shape=(tile,) * (NSEND + 1),
        in_specs=[SM, SM] + [VM] * 11,
        out_specs=(VM,) * (NSEND + 1),
        scratch_shapes=SCRATCH
        + [pltpu.VMEM((TILES, EDGE, EDGE, BZ), f32), pltpu.SMEM((TILES,), jnp.int32)],
        compiler_params=PARAMS,
        name="final",
    )(tissue, gives, est, own, *halos, wx, wy, wz)


def store_kernel(takes, *refs):
    arrived, out, sems = refs[: NSEND + 1], refs[NSEND + 1], refs[NSEND + 2]

    def copy(c):
        return pltpu.make_async_copy(arrived[c], out.at[jnp.maximum(takes[c], 0)], sems.at[c])

    for c in range(NSEND + 1):

        @pl.when(takes[c] >= 0)
        def _(c=c):
            copy(c).start()

    for c in range(NSEND + 1):

        @pl.when(takes[c] >= 0)
        def _(c=c):
            copy(c).wait()


def store_call(takes, arrived):
    any_spec = pl.BlockSpec(memory_space=pl.ANY)
    return pl.pallas_call(
        store_kernel,
        out_shape=jax.ShapeDtypeStruct((CAP, EDGE, EDGE, BZ), f32),
        in_specs=[SM] + [any_spec] * (NSEND + 1),
        out_specs=any_spec,
        scratch_shapes=[pltpu.SemaphoreType.DMA((NSEND + 1,))],
        compiler_params=PARAMS,
        name="store",
    )(takes, *arrived)


def shift(values, axis, step):
    count = lax.axis_size(axis)
    return lax.ppermute(
        values, axis, [(i, i + step) for i in range(count) if 0 <= i + step < count]
    )


def exchange(xs_lo, xs_hi, ys_lo, ys_hi):
    ym = shift(ys_hi, "owner", 1)
    yp = shift(ys_lo, "owner", -1)
    xm = shift(xs_hi, "slab", 1)
    xp = shift(xs_lo, "slab", -1)
    sides = jnp.concatenate([ym, yp], axis=1)
    cm = shift(sides[BX - HALF :], "slab", 1)
    cp = shift(sides[:HALF], "slab", -1)
    return xm, xp, ym, yp, cm, cp


def body(observed, tissue, point_spread):
    wx, wy, wz = make_weights(point_spread)
    me = lax.axis_index("owner")
    gives = jnp.asarray(GIVES, jnp.int32)[me]
    takes = jnp.asarray(TAKES, jnp.int32)[me]
    spread, *edges = first_call(tissue, observed, wz)
    ratio, *edges = ratio_call(tissue, observed, spread, exchange(*edges), wx, wy)
    est, spread, *edges = update_call(tissue, observed, ratio, exchange(*edges), wx, wy, wz)
    ratio, *edges = ratio_call(tissue, observed, spread, exchange(*edges), wx, wy)
    *sends, keep = final_call(tissue, gives, est, ratio, exchange(*edges), wx, wy, wz)
    arrived = [
        lax.ppermute(send, "owner", [(e[0], e[1]) for e in step])
        for send, step in zip(sends, SENDS)
    ]
    return store_call(takes, arrived + [keep])


def solution(mesh):
    in_specs = (P("slab", "owner", None), P("slab", "owner"), P())
    out_specs = P(("slab", "owner"), None, None, None)
    return jax.shard_map(body, mesh=mesh, in_specs=in_specs, out_specs=out_specs, check_vma=False)
```

```python
import jax
import jax.numpy as jnp
from jax import lax
from jax.experimental import pallas as pl
from jax.experimental.pallas import tpu as pltpu
from jax.sharding import PartitionSpec as P

ITERS = 2
ratio_floor = 0.05

BX, BY, BZ = 64, 128, 128
TAPS, HALF = 33, 16
EDGE = 32
TILES = 8
CAP = 7
OWNERS = 16
MID = BY - 2 * HALF
WIDE = 6

bf16 = jnp.bfloat16
f32 = jnp.float32
VM = pl.BlockSpec(memory_space=pltpu.VMEM)
SM = pl.BlockSpec(memory_space=pltpu.SMEM)
PARAMS = pltpu.CompilerParams(vmem_limit_bytes=14 << 20)


GROUP = (("e", 0), ("m", 0), ("m", 16), ("e", 16))


def first_rank(c):
    return 7 * c if c % 2 == 0 else 7 * (c - 1) + 8


def tile_edges():
    out = []
    for c in range(OWNERS):
        for k in range(8 if c % 2 == 0 else 6):
            rank = first_rank(c) + k
            out.append((c, rank % OWNERS, k, rank // OWNERS))
    return out


def colour(edges):
    colours = max(
        max(sum(e[0] == v for e in edges), sum(e[1] == v for e in edges)) for v in range(OWNERS)
    )
    at_src = [[None] * colours for _ in range(OWNERS)]
    at_dst = [[None] * colours for _ in range(OWNERS)]
    for e in edges:
        s, d = e[0], e[1]
        a = at_src[s].index(None)
        b = at_dst[d].index(None)
        if a != b and at_dst[d][a] is not None:
            path, side, v, c = [], "d", d, a
            while True:
                nxt = (at_dst if side == "d" else at_src)[v][c]
                if nxt is None:
                    break
                path.append((nxt, c))
                v = nxt[0] if side == "d" else nxt[1]
                side = "s" if side == "d" else "d"
                c = b if c == a else a
            for edge, c in path:
                at_src[edge[0]][c] = None
                at_dst[edge[1]][c] = None
            for edge, c in path:
                n = b if c == a else a
                at_src[edge[0]][n] = edge
                at_dst[edge[1]][n] = edge
        at_src[s][a] = e
        at_dst[d][a] = e
    return [[at_src[s][c] for s in range(OWNERS) if at_src[s][c] is not None] for c in range(colours)]


EDGES = tile_edges()
SENDS = colour([e for e in EDGES if e[0] != e[1]])
NSEND = len(SENDS)
GIVES = [[0] * (NSEND + 1) for _ in range(OWNERS)]
TAKES = [[-1] * (NSEND + 1) for _ in range(OWNERS)]
for _c, _step in enumerate(SENDS + [[e for e in EDGES if e[0] == e[1]]]):
    for _e in _step:
        GIVES[_e[0]][_c] = _e[2]
        TAKES[_e[1]][_c] = _e[3]


def parts(values):
    high = values.astype(bf16)
    return high, (values - high.astype(f32)).astype(bf16)


def weight_kernel(taps_ref, rows_ref, x_ref, y_ref, e_ref, z_ref):
    total = jnp.sum(rows_ref[...], axis=1, keepdims=True)

    def band(axis, distance, flip):
        acc = jnp.zeros(distance.shape, f32)
        for k in range(TAPS):
            tap = taps_ref[axis, TAPS - 1 - k if flip else k]
            acc = jnp.where(distance == k, tap, acc)
        return acc / total[axis : axis + 1, :]

    def grid(rows, cols):
        return (
            lax.broadcasted_iota(jnp.int32, (rows, cols), 0),
            lax.broadcasted_iota(jnp.int32, (rows, cols), 1),
        )

    for flip in (0, 1):
        r, c = grid(128, 384)
        high, low = parts(band(0, jnp.where((r % 8) == (c % 8), c // 8 - r // 8, -1), flip))
        x_ref[flip, :, 0:384] = high
        x_ref[flip, :, 384:768] = high
        x_ref[flip, :, 768:1152] = low
        r, c = grid(MID, BY)
        high, low = parts(band(1, c - r, flip))
        y_ref[flip, :, 0:128] = high
        y_ref[flip, :, 128:256] = high
        y_ref[flip, :, 256:384] = low
        r, c = grid(64, 192)
        p = c - 48 * ((c >= 48).astype(jnp.int32) + (c >= 96) + (c >= 144))
        side = jnp.where(c >= 96, c - 96, c) >= 48
        same = ((r & 16) > 0) == side
        both = band(1, jnp.where(same, p - (r & 15), -1), flip)
        high, low = parts(both)
        rest = jnp.where(c < 96, low.astype(f32), 0.0)
        e_ref[flip] = jnp.where(r < 32, high.astype(f32), rest).astype(bf16)
        r, c = grid(BZ, BZ)
        high, low = parts(band(2, r - c + HALF, flip))
        z_ref[flip, 0:128, 0:128] = high
        z_ref[flip, 128:256, 0:128] = high
        z_ref[flip, 0:128, 128:256] = low
        z_ref[flip, 128:256, 128:256] = jnp.zeros((128, 128), bf16)


def neighbours():
    row, me = lax.axis_index("slab"), lax.axis_index("owner")
    ends = [row > 0, row < lax.axis_size("slab") - 1, me > 0, me < lax.axis_size("owner") - 1]
    return [jnp.where(end, 1.0, 0.0).astype(f32) for end in ends]


def call(kernel, name, outs, scratch, small, arrays, micros=1.0):
    cost = pl.CostEstimate(
        flops=int(1.1e9 * micros), bytes_accessed=int(3.6e6 * micros), transcendentals=0
    )
    return pl.pallas_call(
        kernel,
        cost_estimate=cost,
        out_shape=tuple(outs),
        in_specs=[SM] * len(small) + [VM] * len(arrays),
        out_specs=(VM,) * len(outs),
        scratch_shapes=scratch,
        compiler_params=PARAMS,
        name=name,
    )(*small, *arrays)


def arr(*shape, dtype=f32):
    return jax.ShapeDtypeStruct(shape, dtype)


def make_weights(point_spread):
    outs = [
        arr(2, 128, 1152, dtype=bf16),
        arr(2, MID, 384, dtype=bf16),
        arr(2, 64, 192, dtype=bf16),
        arr(2, 256, 256, dtype=bf16),
    ]
    return call(weight_kernel, "weights", outs, [], [point_spread], [point_spread])


def z_pass(rows, weights):
    high, low = parts(rows)
    both = jnp.dot(jnp.concatenate([high, low], axis=1), weights, preferred_element_type=f32)
    return both[:, :128] + both[:, 128:]


def keep(out, lines, row0, high_ref, low_ref):
    octets = out.shape[0] // 8
    out = jnp.concatenate(
        [out[:, 128 * i : 128 * i + 128].reshape(octets, 8, 128) for i in range(lines)], axis=1
    )
    high, low = parts(out)
    rows = pl.ds(pl.multiple_of(row0 * 8, 64), 8 * lines)
    high_ref[:, rows, :] = high
    low_ref[:, rows, :] = low


def y_mid(lines, weights, row0, high_ref, low_ref):
    high, low = parts(jnp.concatenate(lines, axis=1))
    out = jnp.dot(weights, jnp.concatenate([high, low, high], axis=0), preferred_element_type=f32)
    keep(out, len(lines), row0, high_ref, low_ref)


def y_edges(lines, weights, row0, high_ref, low_ref):
    high, low = parts(jnp.concatenate(lines, axis=1))
    out = jnp.dot(weights, jnp.concatenate([high, low], axis=0), preferred_element_type=f32)
    keep(out[:32] + out[32:], len(lines), row0, high_ref, low_ref)


def each_eight(rows, line, use):
    def step(i, carry):
        use([line(i * 8 + k) for k in range(8)], i * 8)
        return carry

    lax.fori_loop(0, rows // 8, step, 0, unroll=True)


def own_rows(make, use):
    each_eight(16, lambda r: make("e", r), lambda lines, r: use(lines, r))
    each_eight(32, lambda r: make("m", r), lambda lines, r: use(lines, r + 16))
    each_eight(16, lambda r: make("e", r + 16), lambda lines, r: use(lines, r + 48))


def x_dot(weights, high, low):
    return jnp.dot(
        weights, jnp.concatenate([high, low, high], axis=0), preferred_element_type=f32
    )


def split_lanes(out, count):
    return [out[:, 128 * i : 128 * i + 128] for i in range(count)]


def get(ref, row, octet):
    col = octet * 8 if isinstance(octet, int) else pl.multiple_of(octet * 8, 8)
    return ref[row : row + 16, pl.ds(col, 8), :].reshape(128, 128)


def put(ref, row, octet, piece):
    col = octet * 8 if isinstance(octet, int) else pl.multiple_of(octet * 8, 8)
    ref[row : row + 16, pl.ds(col, 8), :] = piece.reshape(16, 8, 128)


def masked_piece(observed, tissue, g, octet):
    return get(observed, 16 * g, octet) * tissue[g // 2, octet // 4].astype(f32)


def finish(kind, z_ref, pieces, bases):
    if kind == "ratio":
        return [[base / jnp.maximum(p, ratio_floor) for p, base in zip(pieces, bases)]]
    factor = z_pass(jnp.concatenate(pieces, axis=0), z_ref[1])
    new = jnp.concatenate(bases, axis=0) * factor
    fields = [new] if kind == "final" else [new, z_pass(new, z_ref[0])]
    return [
        [field[128 * i : 128 * i + 128] for i in range(len(pieces))] for field in fields
    ]


def count_out(kind):
    return 2 if kind == "update" else 1


def flip_of(kind):
    return 0 if kind == "ratio" else 1


def mid_finish(kind, tissue, base, z_ref, outs, g, o0, pieces):
    row = GROUP[g][1]
    bases = [
        get(base, row, o0 + i)
        if kind == "final"
        else masked_piece(base, tissue, g, o0 + i + 2)
        for i in range(WIDE)
    ]
    for ref, field in zip(outs, finish(kind, z_ref, pieces, bases)):
        for i in range(WIDE):
            put(ref, row, o0 + i, field[i])


EDGE_OCTETS = (0, 1, 14, 15)


def edge_finish(kind, tissue, base, z_ref, outs, g, pieces):
    row = GROUP[g][1]
    bases = [
        get(base[i // 2], row, i % 2)
        if kind == "final"
        else masked_piece(base[0], tissue, g, EDGE_OCTETS[i])
        for i in range(4)
    ]
    for refs, field in zip(outs, finish(kind, z_ref, pieces, bases)):
        for i in range(4):
            put(refs[i // 2], row, i % 2, field[i])


def kernel_a(kind):
    def run(tissue, base, lo_m, lo_e, mid_m, mid_e, hi_m, hi_e, x_ref, y_ref, z_ref, *outs):
        outs, (high_ref, low_ref) = outs[:-2], outs[-2:]
        flip = flip_of(kind)
        own = {"m": (lo_m, mid_m, hi_m), "e": (lo_e, mid_e, hi_e)}
        own_rows(
            lambda part, r: jnp.concatenate([ref[r] for ref in own[part]], axis=0),
            lambda lines, x: y_mid(lines, y_ref[flip], x, high_ref, low_ref),
        )

        def step(q, carry):
            o0 = q * WIDE
            for g in (1, 2):
                rows = slice(128 * (g - 1), 128 * (g - 1) + 384)
                high = jnp.concatenate([high_ref[o0 + i, rows] for i in range(WIDE)], axis=1)
                low = jnp.concatenate([low_ref[o0 + i, rows] for i in range(WIDE)], axis=1)
                pieces = split_lanes(x_dot(x_ref[flip], high, low), WIDE)
                mid_finish(kind, tissue, base, z_ref, outs, g, o0, pieces)
            return carry

        lax.fori_loop(0, MID // 8 // WIDE, step, 0, unroll=True)

    return run


def kernel_b(kind):
    def run(tissue, base, xm, xp, own_high, own_low, x_ref, y_ref, z_ref, *outs):
        outs, (high_ref, low_ref) = outs[:-2], outs[-2:]
        flip, inside = flip_of(kind), neighbours()
        for halo, near, row0 in ((xm, inside[0], 0), (xp, inside[1], 16)):
            each_eight(
                16,
                lambda r, halo=halo, near=near: halo[r] * near,
                lambda lines, r, row0=row0: y_mid(
                    lines, y_ref[flip], r + row0, high_ref, low_ref
                ),
            )

        def step(q, carry):
            o0 = q * WIDE
            for g in (0, 3):

                def rows(halo_ref, own_ref):
                    if g == 0:
                        both = [
                            jnp.concatenate(
                                [halo_ref[o0 + i, 0:128], own_ref[o0 + i, 0:256]], axis=0
                            )
                            for i in range(WIDE)
                        ]
                    else:
                        both = [
                            jnp.concatenate(
                                [own_ref[o0 + i, 256:512], halo_ref[o0 + i, 128:256]], axis=0
                            )
                            for i in range(WIDE)
                        ]
                    return jnp.concatenate(both, axis=1)

                out = x_dot(x_ref[flip], rows(high_ref, own_high), rows(low_ref, own_low))
                mid_finish(kind, tissue, base, z_ref, outs, g, o0, split_lanes(out, WIDE))
            return carry

        lax.fori_loop(0, MID // 8 // WIDE, step, 0, unroll=True)

    return run


def kernel_c(kind):
    def run(tissue, *refs):
        nbase = 2 if kind == "final" else 1
        base, refs = refs[:nbase], refs[nbase:]
        (ym_m, ym_e, yp_m, yp_e, lo_m, lo_e, mid_m, mid_e, hi_m, hi_e), refs = refs[:10], refs[10:]
        (x_ref, e_ref, z_ref), refs = refs[:3], refs[3:]
        outs, (high_ref, low_ref) = refs[:-2], refs[-2:]
        flip, inside = flip_of(kind), neighbours()
        own = {"m": (ym_m, lo_m, mid_m, hi_m, yp_m), "e": (ym_e, lo_e, mid_e, hi_e, yp_e)}

        def line(part, r):
            ym, lo, mid, hi, yp = own[part]
            return jnp.concatenate(
                [
                    ym[r] * inside[2],
                    lo[r],
                    mid[r, :HALF],
                    mid[r, MID - HALF :],
                    hi[r],
                    yp[r] * inside[3],
                ],
                axis=0,
            )

        own_rows(line, lambda lines, x: y_edges(lines, e_ref[flip], x, high_ref, low_ref))
        for g in (1, 2):
            rows = slice(128 * (g - 1), 128 * (g - 1) + 384)
            high = jnp.concatenate([high_ref[i, rows] for i in range(4)], axis=1)
            low = jnp.concatenate([low_ref[i, rows] for i in range(4)], axis=1)
            pieces = split_lanes(x_dot(x_ref[flip], high, low), 4)
            pairs = [outs[2 * f : 2 * f + 2] for f in range(count_out(kind))]
            edge_finish(kind, tissue, base, z_ref, pairs, g, pieces)

    return run


def edge_d(kind, tissue, base, xm, xp, cm, cp, own_high, own_low, x_ref, e_ref, z_ref, pairs, high_ref, low_ref):
    flip, inside = flip_of(kind), neighbours()
    for halo, corner, near, row0 in ((xm, cm, inside[0], 0), (xp, cp, inside[1], 16)):

        def line(r, halo=halo, corner=corner, near=near):
            return jnp.concatenate(
                [
                    corner[r, :HALF] * (near * inside[2]),
                    halo[r, : 2 * HALF] * near,
                    halo[r, BY - 2 * HALF :] * near,
                    corner[r, HALF:] * (near * inside[3]),
                ],
                axis=0,
            )

        each_eight(
            16,
            line,
            lambda lines, r, row0=row0: y_edges(lines, e_ref[flip], r + row0, high_ref, low_ref),
        )
    for g in (0, 3):

        def rows(halo_ref, own_ref):
            if g == 0:
                both = [
                    jnp.concatenate([halo_ref[i, 0:128], own_ref[i, 0:256]], axis=0)
                    for i in range(4)
                ]
            else:
                both = [
                    jnp.concatenate([own_ref[i, 256:512], halo_ref[i, 128:256]], axis=0)
                    for i in range(4)
                ]
            return jnp.concatenate(both, axis=1)

        out = x_dot(x_ref[flip], rows(high_ref, own_high), rows(low_ref, own_low))
        edge_finish(kind, tissue, base, z_ref, pairs, g, split_lanes(out, 4))


def fill_strips(mid_e, lo_e, hi_e, xs_lo, xs_hi):
    for ref, row in ((xs_lo, 0), (xs_hi, 16)):
        ref[:, :HALF, :] = lo_e[row : row + 16]
        ref[:, HALF : BY - HALF, :] = mid_e[row : row + 16]
        ref[:, BY - HALF :, :] = hi_e[row : row + 16]


def kernel_d(kind):
    def run(tissue, base, xm, xp, cm, cp, own_high, own_low, mid_e, x_ref, e_ref, z_ref, *outs):
        outs, (xs_lo, xs_hi, high_ref, low_ref) = outs[:-4], outs[-4:]
        pairs = [outs[2 * f : 2 * f + 2] for f in range(count_out(kind))]
        edge_d(
            kind, tissue, (base,), xm, xp, cm, cp, own_high, own_low,
            x_ref, e_ref, z_ref, pairs, high_ref, low_ref,
        )
        fill_strips(mid_e, *pairs[-1], xs_lo, xs_hi)

    return run


def kernel_last(tissue, gives, base_lo, base_hi, xm, xp, cm, cp, own_high, own_low, mid_m, mid_e, lo_m, hi_m, x_ref, e_ref, z_ref, *refs):
    sends, (lo_e, hi_e, high_ref, low_ref, tiles, nth) = refs[: NSEND + 1], refs[NSEND + 1 :]
    for t in range(TILES):
        nth[t] = 0
    count = jnp.int32(0)
    for t in range(TILES):
        flag = tissue[t // 4, t % 4]

        @pl.when(flag > 0)
        def _(t=t, count=count):
            nth[count] = t

        count = count + (flag > 0).astype(jnp.int32)
    edge_d(
        "final", tissue, (base_lo, base_hi), xm, xp, cm, cp, own_high, own_low,
        x_ref, e_ref, z_ref, [(lo_e, hi_e)], high_ref, low_ref,
    )
    for i in range(2):
        for (lo, mid, hi), row, half in (
            ((lo_e, mid_e, hi_e), 16 * i, 16 * i),
            ((lo_m, mid_m, hi_m), 16 * i, 16 * (1 - i)),
        ):
            rows, into = slice(row, row + 16), slice(half, half + 16)
            tiles[4 * i, into, :HALF] = lo[rows]
            tiles[4 * i, into, HALF:] = mid[rows, :HALF]
            tiles[4 * i + 1, into] = mid[rows, HALF : HALF + EDGE]
            tiles[4 * i + 2, into] = mid[rows, HALF + EDGE : HALF + 2 * EDGE]
            tiles[4 * i + 3, into, :HALF] = mid[rows, MID - HALF :]
            tiles[4 * i + 3, into, HALF:] = hi[rows]
    for c, send in enumerate(sends):
        send[...] = tiles[nth[gives[lax.axis_index("owner"), c]]]


def first_kernel(tissue, observed, z_ref, lo_m, lo_e, mid_m, mid_e, hi_m, hi_e, xs_lo, xs_hi):
    mids, edges = {"m": mid_m, "e": mid_e}, {"m": (lo_m, hi_m), "e": (lo_e, hi_e)}
    for g, (part, row) in enumerate(GROUP):

        def step(q, carry, g=g, part=part, row=row):
            o0 = q * WIDE
            pieces = [masked_piece(observed, tissue, g, o0 + i + 2) for i in range(WIDE)]
            done = z_pass(jnp.concatenate(pieces, axis=0), z_ref[0])
            for i in range(WIDE):
                put(mids[part], row, o0 + i, done[128 * i : 128 * i + 128])
            return carry

        lax.fori_loop(0, MID // 8 // WIDE, step, 0, unroll=True)
        pieces = [masked_piece(observed, tissue, g, o) for o in EDGE_OCTETS]
        done = z_pass(jnp.concatenate(pieces, axis=0), z_ref[0])
        for i in range(4):
            put(edges[part][i // 2], row, i % 2, done[128 * i : 128 * i + 128])
    fill_strips(mid_e, lo_e, hi_e, xs_lo, xs_hi)


EDGE_PART = arr(32, HALF, BZ)
MID_PART = arr(32, MID, BZ)
X_STRIP = arr(HALF, BY, BZ)
TILE_ARR = arr(EDGE, EDGE, BZ)


def own_parts(octets):
    return [arr(octets, 8 * BX, 128, dtype=bf16)] * 2


def halo_parts(octets):
    return [pltpu.VMEM((octets, 8 * 2 * HALF, 128), bf16)] * 2


def blur(kind, tissue, gives, base, field, weights):
    lo_m, lo_e, mid_m, mid_e, hi_m, hi_e, xs_lo, xs_hi = field
    wx, wy, we, wz = weights
    count = count_out(kind)
    ym_e = shift(hi_e, "owner", 1)
    yp_e = shift(lo_e, "owner", -1)
    xm = shift(xs_hi, "slab", 1)
    xp = shift(xs_lo, "slab", -1)
    ym_m = shift(hi_m, "owner", 1)
    yp_m = shift(lo_m, "owner", -1)
    if kind == "final":
        base_lo_m, base_lo_e, base_mid_m, base_mid_e, base_hi_m, base_hi_e = base
        base_c, base_d = [base_lo_m, base_hi_m], [base_lo_e, base_hi_e]
    else:
        base_mid_m = base_mid_e = base
        base_c = base_d = [base]
    own = [lo_m, lo_e, mid_m, mid_e, hi_m, hi_e]
    *new_mid_m, high, low = call(
        kernel_a(kind), kind + "_a", [MID_PART] * count + own_parts(MID // 8), [],
        [tissue], [base_mid_m, *own, wx, wy, wz], 4.0,
    )
    cm = shift(jnp.concatenate([ym_e[16:], yp_e[16:]], axis=1), "slab", 1)
    cp = shift(jnp.concatenate([ym_e[:16], yp_e[:16]], axis=1), "slab", -1)
    new_mid_e = call(
        kernel_b(kind), kind + "_b", [MID_PART] * count, halo_parts(MID // 8),
        [tissue], [base_mid_e, xm, xp, high, low, wx, wy, wz], 3.0,
    )
    *new_m, edge_high, edge_low = call(
        kernel_c(kind), kind + "_c", [EDGE_PART] * (2 * count) + own_parts(4), [],
        [tissue], [*base_c, ym_m, ym_e, yp_m, yp_e, *own, wx, we, wz], 2.0,
    )
    late = [xm, xp, cm, cp, edge_high, edge_low]
    if kind == "final":
        scratch = [pltpu.VMEM((32, HALF, BZ), f32)] * 2 + halo_parts(4)
        scratch += [pltpu.VMEM((TILES, EDGE, EDGE, BZ), f32), pltpu.SMEM((TILES,), jnp.int32)]
        return call(
            kernel_last, "final_d", [TILE_ARR] * (NSEND + 1), scratch,
            [tissue, gives],
            [*base_d, *late, new_mid_m[0], new_mid_e[0], *new_m, wx, we, wz], 2.0,
        )
    *new_e, xs_lo, xs_hi = call(
        kernel_d(kind), kind + "_d", [EDGE_PART] * (2 * count) + [X_STRIP] * 2, halo_parts(4),
        [tissue], [*base_d, *late, new_mid_e[-1], wx, we, wz], 2.0,
    )
    fields = [
        [
            new_m[2 * f], new_e[2 * f], new_mid_m[f], new_mid_e[f], new_m[2 * f + 1],
            new_e[2 * f + 1],
        ]
        for f in range(count)
    ]
    return fields[:-1] + [fields[-1] + [xs_lo, xs_hi]]


def store_kernel(takes, *refs):
    arrived, out, sems = refs[: NSEND + 1], refs[NSEND + 1], refs[NSEND + 2]
    me = lax.axis_index("owner")

    def copy(c):
        return pltpu.make_async_copy(arrived[c], out.at[jnp.maximum(takes[me, c], 0)], sems.at[c])

    for c in range(NSEND + 1):

        @pl.when(takes[me, c] >= 0)
        def _(c=c):
            copy(c).start()

    for c in range(NSEND + 1):

        @pl.when(takes[me, c] >= 0)
        def _(c=c):
            copy(c).wait()


def store_call(takes, arrived):
    any_spec = pl.BlockSpec(memory_space=pl.ANY)
    return pl.pallas_call(
        store_kernel,
        out_shape=jax.ShapeDtypeStruct((CAP, EDGE, EDGE, BZ), f32),
        in_specs=[SM] + [any_spec] * (NSEND + 1),
        out_specs=any_spec,
        scratch_shapes=[pltpu.SemaphoreType.DMA((NSEND + 1,))],
        compiler_params=PARAMS,
        name="store",
    )(takes, *arrived)


def shift(values, axis, step):
    count = lax.axis_size(axis)
    return lax.ppermute(values, axis, [(i, (i + step) % count) for i in range(count)])


def body(observed, tissue, point_spread):
    weights = make_weights(point_spread)
    gives = jnp.asarray(GIVES, jnp.int32)
    takes = jnp.asarray(TAKES, jnp.int32)
    outs = [EDGE_PART] * 2 + [MID_PART] * 2 + [EDGE_PART] * 2 + [X_STRIP] * 2
    field = call(first_kernel, "first", outs, [], [tissue], [observed, weights[3]])
    base = observed
    for iteration in range(ITERS):
        (field,) = blur("ratio", tissue, gives, observed, field, weights)
        if iteration < ITERS - 1:
            base, field = blur("update", tissue, gives, base, field, weights)
    *sends, kept = blur("final", tissue, gives, base, field, weights)
    arrived = [
        lax.ppermute(send, "owner", [(e[0], e[1]) for e in step])
        for send, step in zip(sends, SENDS)
    ]
    return store_call(takes, arrived + [kept])


def solution(mesh):
    in_specs = (P("slab", "owner", None), P("slab", "owner"), P())
    out_specs = P(("slab", "owner"), None, None, None)
    return jax.shard_map(body, mesh=mesh, in_specs=in_specs, out_specs=out_specs, check_vma=False)
```

```python
import jax
import jax.numpy as jnp
from jax import lax
from jax.experimental import pallas as pl
from jax.experimental.pallas import tpu as pltpu
from jax.sharding import PartitionSpec as P

ITERS = 2
ratio_floor = 0.05

BX, BY, BZ = 64, 128, 128
TAPS, HALF = 33, 16
EDGE = 32
TILES = 8
CAP = 7
OWNERS = 16
MID = BY - 2 * HALF
WIDE = 6

bf16 = jnp.bfloat16
f32 = jnp.float32
VM = pl.BlockSpec(memory_space=pltpu.VMEM)
SM = pl.BlockSpec(memory_space=pltpu.SMEM)
PARAMS = pltpu.CompilerParams(vmem_limit_bytes=14 << 20)


GROUP = (("e", 0), ("m", 0), ("m", 16), ("e", 16))


def first_rank(c):
    return 7 * c if c % 2 == 0 else 7 * (c - 1) + 8


def tile_edges():
    out = []
    for c in range(OWNERS):
        for k in range(8 if c % 2 == 0 else 6):
            rank = first_rank(c) + k
            out.append((c, rank % OWNERS, k, rank // OWNERS))
    return out


ROUTES = (
    (6, 11, 0, 9, 2, 7, 12, 5, 14, 3, 8, 1, 10, 15, 4, 13),
    (7, 9, 4, 10, 14, 8, 13, 3, 11, 1, 12, 2, 6, 0, 5, -1),
    (2, 8, 1, 11, 15, 9, 0, 6, 10, 4, 13, 3, 5, 14, 7, 12),
    (3, 12, 5, 6, 13, -1, 11, 2, 15, 0, 7, 14, 9, 1, 8, 10),
    (5, 10, 15, 8, 3, 4, 1, -1, 13, 2, 11, 0, 7, 12, 9, 14),
    (4, -1, 14, -1, 1, 6, 15, -1, 12, 5, 9, -1, 8, -1, 3, 11),
    (1, 13, 3, 7, 0, -1, 10, 4, 9, -1, 6, 15, 11, -1, 2, -1),
    (-1, -1, -1, -1, 12, -1, 14, -1, -1, -1, -1, -1, 4, -1, 6, -1),
)
EDGES = tile_edges()
SENDS = [[e for e in EDGES if e[0] != e[1] and to[e[0]] == e[1]] for to in ROUTES]
NSEND = len(SENDS)
assert sum(map(len, SENDS)) + sum(e[0] == e[1] for e in EDGES) == len(EDGES)
GIVES = [[0] * (NSEND + 1) for _ in range(OWNERS)]
TAKES = [[-1] * (NSEND + 1) for _ in range(OWNERS)]
for _c, _step in enumerate(SENDS + [[e for e in EDGES if e[0] == e[1]]]):
    for _e in _step:
        GIVES[_e[0]][_c] = _e[2]
        TAKES[_e[1]][_c] = _e[3]


def parts(values):
    high = values.astype(bf16)
    return high, (values - high.astype(f32)).astype(bf16)


def weight_kernel(taps_ref, rows_ref, x_ref, y_ref, e_ref, z_ref):
    total = jnp.sum(rows_ref[...], axis=1, keepdims=True)

    def band(axis, distance, flip):
        acc = jnp.zeros(distance.shape, f32)
        for k in range(TAPS):
            tap = taps_ref[axis, TAPS - 1 - k if flip else k]
            acc = jnp.where(distance == k, tap, acc)
        return acc / total[axis : axis + 1, :]

    def grid(rows, cols):
        return (
            lax.broadcasted_iota(jnp.int32, (rows, cols), 0),
            lax.broadcasted_iota(jnp.int32, (rows, cols), 1),
        )

    for flip in (0, 1):
        r, c = grid(128, 384)
        high, low = parts(band(0, jnp.where((r % 8) == (c % 8), c // 8 - r // 8, -1), flip))
        x_ref[flip, :, 0:384] = high
        x_ref[flip, :, 384:768] = high
        x_ref[flip, :, 768:1152] = low
        r, c = grid(MID, BY)
        high, low = parts(band(1, c - r, flip))
        y_ref[flip, :, 0:128] = high
        y_ref[flip, :, 128:256] = high
        y_ref[flip, :, 256:384] = low
        r, c = grid(64, 192)
        p = c - 48 * ((c >= 48).astype(jnp.int32) + (c >= 96) + (c >= 144))
        side = jnp.where(c >= 96, c - 96, c) >= 48
        same = ((r & 16) > 0) == side
        both = band(1, jnp.where(same, p - (r & 15), -1), flip)
        high, low = parts(both)
        rest = jnp.where(c < 96, low.astype(f32), 0.0)
        e_ref[flip] = jnp.where(r < 32, high.astype(f32), rest).astype(bf16)
        r, c = grid(BZ, BZ)
        high, low = parts(band(2, r - c + HALF, flip))
        z_ref[flip, 0:128, 0:128] = high
        z_ref[flip, 128:256, 0:128] = high
        z_ref[flip, 0:128, 128:256] = low
        z_ref[flip, 128:256, 128:256] = jnp.zeros((128, 128), bf16)


def neighbours():
    row, me = lax.axis_index("slab"), lax.axis_index("owner")
    ends = [row > 0, row < lax.axis_size("slab") - 1, me > 0, me < lax.axis_size("owner") - 1]
    return [jnp.where(end, 1.0, 0.0).astype(f32) for end in ends]


def call(kernel, name, outs, scratch, small, arrays, micros=1.0):
    cost = pl.CostEstimate(
        flops=int(1.1e9 * micros), bytes_accessed=int(3.6e6 * micros), transcendentals=0
    )
    return pl.pallas_call(
        kernel,
        cost_estimate=cost,
        out_shape=tuple(outs),
        in_specs=[SM] * len(small) + [VM] * len(arrays),
        out_specs=(VM,) * len(outs),
        scratch_shapes=scratch,
        compiler_params=PARAMS,
        name=name,
    )(*small, *arrays)


def arr(*shape, dtype=f32):
    return jax.ShapeDtypeStruct(shape, dtype)


def make_weights(point_spread):
    outs = [
        arr(2, 128, 1152, dtype=bf16),
        arr(2, MID, 384, dtype=bf16),
        arr(2, 64, 192, dtype=bf16),
        arr(2, 256, 256, dtype=bf16),
    ]
    return call(weight_kernel, "weights", outs, [], [point_spread], [point_spread])


def z_pass(rows, weights):
    high, low = parts(rows)
    both = jnp.dot(jnp.concatenate([high, low], axis=1), weights, preferred_element_type=f32)
    return both[:, :128] + both[:, 128:]


def keep(out, lines, row0, high_ref, low_ref):
    octets = out.shape[0] // 8
    out = jnp.concatenate(
        [out[:, 128 * i : 128 * i + 128].reshape(octets, 8, 128) for i in range(lines)], axis=1
    )
    high, low = parts(out)
    rows = pl.ds(pl.multiple_of(row0 * 8, 64), 8 * lines)
    high_ref[:, rows, :] = high
    low_ref[:, rows, :] = low


def y_mid(lines, weights, row0, high_ref, low_ref):
    high, low = parts(jnp.concatenate(lines, axis=1))
    out = jnp.dot(weights, jnp.concatenate([high, low, high], axis=0), preferred_element_type=f32)
    keep(out, len(lines), row0, high_ref, low_ref)


def y_edges(lines, weights, row0, high_ref, low_ref):
    high, low = parts(jnp.concatenate(lines, axis=1))
    out = jnp.dot(weights, jnp.concatenate([high, low], axis=0), preferred_element_type=f32)
    keep(out[:32] + out[32:], len(lines), row0, high_ref, low_ref)


def each_eight(rows, line, use):
    def step(i, carry):
        use([line(i * 8 + k) for k in range(8)], i * 8)
        return carry

    lax.fori_loop(0, rows // 8, step, 0, unroll=True)


def own_rows(make, use):
    each_eight(16, lambda r: make("e", r, r), lambda lines, r: use(lines, r))
    each_eight(32, lambda r: make("m", r, r + 16), lambda lines, r: use(lines, r + 16))
    each_eight(16, lambda r: make("e", r + 16, r + 48), lambda lines, r: use(lines, r + 48))


def x_dot(weights, high, low):
    return jnp.dot(
        weights, jnp.concatenate([high, low, high], axis=0), preferred_element_type=f32
    )


def split_lanes(out, count):
    return [out[:, 128 * i : 128 * i + 128] for i in range(count)]


def get(ref, row, octet):
    col = octet * 8 if isinstance(octet, int) else pl.multiple_of(octet * 8, 8)
    return ref[row : row + 16, pl.ds(col, 8), :].reshape(128, 128)


def put(ref, row, octet, piece):
    col = octet * 8 if isinstance(octet, int) else pl.multiple_of(octet * 8, 8)
    ref[row : row + 16, pl.ds(col, 8), :] = piece.reshape(16, 8, 128)


def masked_piece(observed, tissue, g, octet):
    return get(observed, 16 * g, octet) * tissue[g // 2, octet // 4].astype(f32)


def finish(kind, z_ref, pieces, bases):
    if kind == "ratio":
        return [[base / jnp.maximum(p, ratio_floor) for p, base in zip(pieces, bases)]]
    factor = z_pass(jnp.concatenate(pieces, axis=0), z_ref[1])
    new = jnp.concatenate(bases, axis=0) * factor
    fields = [new] if kind == "final" else [new, z_pass(new, z_ref[0])]
    return [
        [field[128 * i : 128 * i + 128] for i in range(len(pieces))] for field in fields
    ]


def count_out(kind):
    return 2 if kind == "update" else 1


def flip_of(kind):
    return 0 if kind == "ratio" else 1


def mid_finish(kind, tissue, base, z_ref, outs, g, o0, pieces):
    row = GROUP[g][1]
    bases = [
        get(base, row, o0 + i)
        if kind == "final"
        else masked_piece(base, tissue, g, o0 + i + 2)
        for i in range(WIDE)
    ]
    for ref, field in zip(outs, finish(kind, z_ref, pieces, bases)):
        for i in range(WIDE):
            put(ref, row, o0 + i, field[i])


EDGE_OCTETS = (0, 1, 14, 15)


def edge_finish(kind, tissue, base, z_ref, outs, g, pieces):
    row = GROUP[g][1]
    bases = [
        get(base[i // 2], row, i % 2)
        if kind == "final"
        else masked_piece(base[0], tissue, g, EDGE_OCTETS[i])
        for i in range(4)
    ]
    for refs, field in zip(outs, finish(kind, z_ref, pieces, bases)):
        for i in range(4):
            put(refs[i // 2], row, i % 2, field[i])


def kernel_a(kind):
    def run(tissue, base, lo_m, lo_e, mid_m, mid_e, hi_m, hi_e, x_ref, y_ref, z_ref, *outs):
        outs, (high_ref, low_ref) = outs[:-2], outs[-2:]
        flip = flip_of(kind)
        own = {"m": (lo_m, mid_m, hi_m), "e": (lo_e, mid_e, hi_e)}
        own_rows(
            lambda part, r, x: jnp.concatenate([ref[r] for ref in own[part]], axis=0),
            lambda lines, x: y_mid(lines, y_ref[flip], x, high_ref, low_ref),
        )

        def step(q, carry):
            o0 = q * WIDE
            for g in (1, 2):
                rows = slice(128 * (g - 1), 128 * (g - 1) + 384)
                high = jnp.concatenate([high_ref[o0 + i, rows] for i in range(WIDE)], axis=1)
                low = jnp.concatenate([low_ref[o0 + i, rows] for i in range(WIDE)], axis=1)
                pieces = split_lanes(x_dot(x_ref[flip], high, low), WIDE)
                mid_finish(kind, tissue, base, z_ref, outs, g, o0, pieces)
            return carry

        lax.fori_loop(0, MID // 8 // WIDE, step, 0, unroll=True)

    return run


def kernel_b(kind):
    def run(tissue, base, xm, xp, own_high, own_low, x_ref, y_ref, z_ref, *outs):
        outs, (high_ref, low_ref) = outs[:-2], outs[-2:]
        flip, inside = flip_of(kind), neighbours()
        for halo, near, row0 in ((xm, inside[0], 0), (xp, inside[1], 16)):
            each_eight(
                16,
                lambda r, halo=halo, near=near: halo[r] * near,
                lambda lines, r, row0=row0: y_mid(
                    lines, y_ref[flip], r + row0, high_ref, low_ref
                ),
            )

        def step(q, carry):
            o0 = q * WIDE
            for g in (0, 3):

                def rows(halo_ref, own_ref):
                    if g == 0:
                        both = [
                            jnp.concatenate(
                                [halo_ref[o0 + i, 0:128], own_ref[o0 + i, 0:256]], axis=0
                            )
                            for i in range(WIDE)
                        ]
                    else:
                        both = [
                            jnp.concatenate(
                                [own_ref[o0 + i, 256:512], halo_ref[o0 + i, 128:256]], axis=0
                            )
                            for i in range(WIDE)
                        ]
                    return jnp.concatenate(both, axis=1)

                out = x_dot(x_ref[flip], rows(high_ref, own_high), rows(low_ref, own_low))
                mid_finish(kind, tissue, base, z_ref, outs, g, o0, split_lanes(out, WIDE))
            return carry

        lax.fori_loop(0, MID // 8 // WIDE, step, 0, unroll=True)

    return run


def kernel_c(kind):
    def run(tissue, *refs):
        nbase = 2 if kind == "final" else 1
        base, refs = refs[:nbase], refs[nbase:]
        (ym, yp, lo_m, lo_e, mid_m, mid_e, hi_m, hi_e), refs = refs[:8], refs[8:]
        (x_ref, e_ref, z_ref), refs = refs[:3], refs[3:]
        outs, (high_ref, low_ref) = refs[:-2], refs[-2:]
        flip, inside = flip_of(kind), neighbours()
        own = {"m": (lo_m, mid_m, hi_m), "e": (lo_e, mid_e, hi_e)}

        def line(part, r, x):
            lo, mid, hi = own[part]
            return jnp.concatenate(
                [
                    ym[x] * inside[2],
                    lo[r],
                    mid[r, :HALF],
                    mid[r, MID - HALF :],
                    hi[r],
                    yp[x] * inside[3],
                ],
                axis=0,
            )

        own_rows(line, lambda lines, x: y_edges(lines, e_ref[flip], x, high_ref, low_ref))
        for g in (1, 2):
            rows = slice(128 * (g - 1), 128 * (g - 1) + 384)
            high = jnp.concatenate([high_ref[i, rows] for i in range(4)], axis=1)
            low = jnp.concatenate([low_ref[i, rows] for i in range(4)], axis=1)
            pieces = split_lanes(x_dot(x_ref[flip], high, low), 4)
            pairs = [outs[2 * f : 2 * f + 2] for f in range(count_out(kind))]
            edge_finish(kind, tissue, base, z_ref, pairs, g, pieces)

    return run


def edge_d(kind, tissue, base, xm, xp, cm, cp, own_high, own_low, x_ref, e_ref, z_ref, pairs, high_ref, low_ref):
    flip, inside = flip_of(kind), neighbours()
    for halo, corner, near, row0 in ((xm, cm, inside[0], 0), (xp, cp, inside[1], 16)):

        def line(r, halo=halo, corner=corner, near=near):
            return jnp.concatenate(
                [
                    corner[r, :HALF] * (near * inside[2]),
                    halo[r, : 2 * HALF] * near,
                    halo[r, BY - 2 * HALF :] * near,
                    corner[r, HALF:] * (near * inside[3]),
                ],
                axis=0,
            )

        each_eight(
            16,
            line,
            lambda lines, r, row0=row0: y_edges(lines, e_ref[flip], r + row0, high_ref, low_ref),
        )
    for g in (0, 3):

        def rows(halo_ref, own_ref):
            if g == 0:
                both = [
                    jnp.concatenate([halo_ref[i, 0:128], own_ref[i, 0:256]], axis=0)
                    for i in range(4)
                ]
            else:
                both = [
                    jnp.concatenate([own_ref[i, 256:512], halo_ref[i, 128:256]], axis=0)
                    for i in range(4)
                ]
            return jnp.concatenate(both, axis=1)

        out = x_dot(x_ref[flip], rows(high_ref, own_high), rows(low_ref, own_low))
        edge_finish(kind, tissue, base, z_ref, pairs, g, split_lanes(out, 4))


def fill_strips(mid_e, lo_e, hi_e, lo_m, hi_m, xs_lo, xs_hi, ys_lo, ys_hi):
    for ref, ends, middle in ((ys_lo, lo_e, lo_m), (ys_hi, hi_e, hi_m)):
        ref[:16] = ends[:16]
        ref[16:48] = middle[...]
        ref[48:] = ends[16:]
    for ref, row in ((xs_lo, 0), (xs_hi, 16)):
        ref[:, :HALF, :] = lo_e[row : row + 16]
        ref[:, HALF : BY - HALF, :] = mid_e[row : row + 16]
        ref[:, BY - HALF :, :] = hi_e[row : row + 16]


def kernel_d(kind):
    def run(tissue, base, xm, xp, cm, cp, own_high, own_low, mid_e, lo_m, hi_m, x_ref, e_ref, z_ref, *outs):
        outs, edges, (high_ref, low_ref) = outs[:-6], outs[-6:-2], outs[-2:]
        pairs = [outs[2 * f : 2 * f + 2] for f in range(count_out(kind))]
        edge_d(
            kind, tissue, (base,), xm, xp, cm, cp, own_high, own_low,
            x_ref, e_ref, z_ref, pairs, high_ref, low_ref,
        )
        fill_strips(mid_e, *pairs[-1], lo_m, hi_m, *edges)

    return run


def kernel_last(tissue, gives, base_lo, base_hi, xm, xp, cm, cp, own_high, own_low, mid_m, mid_e, lo_m, hi_m, x_ref, e_ref, z_ref, *refs):
    sends, (lo_e, hi_e, high_ref, low_ref, tiles, nth) = refs[: NSEND + 1], refs[NSEND + 1 :]
    for t in range(TILES):
        nth[t] = 0
    count = jnp.int32(0)
    for t in range(TILES):
        flag = tissue[t // 4, t % 4]

        @pl.when(flag > 0)
        def _(t=t, count=count):
            nth[count] = t

        count = count + (flag > 0).astype(jnp.int32)
    edge_d(
        "final", tissue, (base_lo, base_hi), xm, xp, cm, cp, own_high, own_low,
        x_ref, e_ref, z_ref, [(lo_e, hi_e)], high_ref, low_ref,
    )
    for i in range(2):
        for (lo, mid, hi), row, half in (
            ((lo_e, mid_e, hi_e), 16 * i, 16 * i),
            ((lo_m, mid_m, hi_m), 16 * i, 16 * (1 - i)),
        ):
            rows, into = slice(row, row + 16), slice(half, half + 16)
            tiles[4 * i, into, :HALF] = lo[rows]
            tiles[4 * i, into, HALF:] = mid[rows, :HALF]
            tiles[4 * i + 1, into] = mid[rows, HALF : HALF + EDGE]
            tiles[4 * i + 2, into] = mid[rows, HALF + EDGE : HALF + 2 * EDGE]
            tiles[4 * i + 3, into, :HALF] = mid[rows, MID - HALF :]
            tiles[4 * i + 3, into, HALF:] = hi[rows]
    for c, send in enumerate(sends):
        send[...] = tiles[nth[gives[lax.axis_index("owner"), c]]]


def first_kernel(tissue, observed, z_ref, lo_m, lo_e, mid_m, mid_e, hi_m, hi_e, *strips):
    mids, edges = {"m": mid_m, "e": mid_e}, {"m": (lo_m, hi_m), "e": (lo_e, hi_e)}
    for g, (part, row) in enumerate(GROUP):

        def step(q, carry, g=g, part=part, row=row):
            o0 = q * WIDE
            pieces = [masked_piece(observed, tissue, g, o0 + i + 2) for i in range(WIDE)]
            done = z_pass(jnp.concatenate(pieces, axis=0), z_ref[0])
            for i in range(WIDE):
                put(mids[part], row, o0 + i, done[128 * i : 128 * i + 128])
            return carry

        lax.fori_loop(0, MID // 8 // WIDE, step, 0, unroll=True)
        pieces = [masked_piece(observed, tissue, g, o) for o in EDGE_OCTETS]
        done = z_pass(jnp.concatenate(pieces, axis=0), z_ref[0])
        for i in range(4):
            put(edges[part][i // 2], row, i % 2, done[128 * i : 128 * i + 128])
    fill_strips(mid_e, lo_e, hi_e, lo_m, hi_m, *strips)


EDGE_PART = arr(32, HALF, BZ)
MID_PART = arr(32, MID, BZ)
STRIPS = [arr(HALF, BY, BZ)] * 2 + [arr(BX, HALF, BZ)] * 2
TILE_ARR = arr(EDGE, EDGE, BZ)


def own_parts(octets):
    return [arr(octets, 8 * BX, 128, dtype=bf16)] * 2


def halo_parts(octets):
    return [pltpu.VMEM((octets, 8 * 2 * HALF, 128), bf16)] * 2


def blur(kind, tissue, gives, base, field, weights):
    lo_m, lo_e, mid_m, mid_e, hi_m, hi_e, xs_lo, xs_hi, ys_lo, ys_hi = field
    wx, wy, we, wz = weights
    count = count_out(kind)
    ym = shift(ys_hi, "owner", 1)
    yp = shift(ys_lo, "owner", -1)
    xm = shift(xs_hi, "slab", 1)
    xp = shift(xs_lo, "slab", -1)
    if kind == "final":
        base_lo_m, base_lo_e, base_mid_m, base_mid_e, base_hi_m, base_hi_e = base
        base_c, base_d = [base_lo_m, base_hi_m], [base_lo_e, base_hi_e]
    else:
        base_mid_m = base_mid_e = base
        base_c = base_d = [base]
    own = [lo_m, lo_e, mid_m, mid_e, hi_m, hi_e]
    *new_mid_m, high, low = call(
        kernel_a(kind), kind + "_a", [MID_PART] * count + own_parts(MID // 8), [],
        [tissue], [base_mid_m, *own, wx, wy, wz], 4.0,
    )
    cm = shift(jnp.concatenate([ym[BX - HALF :], yp[BX - HALF :]], axis=1), "slab", 1)
    cp = shift(jnp.concatenate([ym[:HALF], yp[:HALF]], axis=1), "slab", -1)
    new_mid_e = call(
        kernel_b(kind), kind + "_b", [MID_PART] * count, halo_parts(MID // 8),
        [tissue], [base_mid_e, xm, xp, high, low, wx, wy, wz], 3.0,
    )
    *new_m, edge_high, edge_low = call(
        kernel_c(kind), kind + "_c", [EDGE_PART] * (2 * count) + own_parts(4), [],
        [tissue], [*base_c, ym, yp, *own, wx, we, wz], 2.0,
    )
    late = [xm, xp, cm, cp, edge_high, edge_low]
    if kind == "final":
        scratch = [pltpu.VMEM((32, HALF, BZ), f32)] * 2 + halo_parts(4)
        scratch += [pltpu.VMEM((TILES, EDGE, EDGE, BZ), f32), pltpu.SMEM((TILES,), jnp.int32)]
        return call(
            kernel_last, "final_d", [TILE_ARR] * (NSEND + 1), scratch,
            [tissue, gives],
            [*base_d, *late, new_mid_m[0], new_mid_e[0], *new_m, wx, we, wz], 2.0,
        )
    *new_e, xs_lo, xs_hi, ys_lo, ys_hi = call(
        kernel_d(kind), kind + "_d", [EDGE_PART] * (2 * count) + STRIPS, halo_parts(4),
        [tissue], [*base_d, *late, new_mid_e[-1], *new_m[-2:], wx, we, wz], 2.0,
    )
    fields = [
        [
            new_m[2 * f], new_e[2 * f], new_mid_m[f], new_mid_e[f], new_m[2 * f + 1],
            new_e[2 * f + 1],
        ]
        for f in range(count)
    ]
    return fields[:-1] + [fields[-1] + [xs_lo, xs_hi, ys_lo, ys_hi]]


def store_kernel(takes, *refs):
    arrived, out, sems = refs[: NSEND + 1], refs[NSEND + 1], refs[NSEND + 2]
    me = lax.axis_index("owner")

    def copy(c):
        return pltpu.make_async_copy(arrived[c], out.at[jnp.maximum(takes[me, c], 0)], sems.at[c])

    for c in range(NSEND + 1):

        @pl.when(takes[me, c] >= 0)
        def _(c=c):
            copy(c).start()

    for c in range(NSEND + 1):

        @pl.when(takes[me, c] >= 0)
        def _(c=c):
            copy(c).wait()


def store_call(takes, arrived):
    any_spec = pl.BlockSpec(memory_space=pl.ANY)
    return pl.pallas_call(
        store_kernel,
        out_shape=jax.ShapeDtypeStruct((CAP, EDGE, EDGE, BZ), f32),
        in_specs=[SM] + [any_spec] * (NSEND + 1),
        out_specs=any_spec,
        scratch_shapes=[pltpu.SemaphoreType.DMA((NSEND + 1,))],
        compiler_params=PARAMS,
        name="store",
    )(takes, *arrived)


def shift(values, axis, step):
    count = lax.axis_size(axis)
    return lax.ppermute(values, axis, [(i, (i + step) % count) for i in range(count)])


def body(observed, tissue, point_spread):
    weights = make_weights(point_spread)
    gives = jnp.asarray(GIVES, jnp.int32)
    takes = jnp.asarray(TAKES, jnp.int32)
    outs = [EDGE_PART] * 2 + [MID_PART] * 2 + [EDGE_PART] * 2 + STRIPS
    field = call(first_kernel, "first", outs, [], [tissue], [observed, weights[3]])
    base = observed
    for iteration in range(ITERS):
        (field,) = blur("ratio", tissue, gives, observed, field, weights)
        if iteration < ITERS - 1:
            base, field = blur("update", tissue, gives, base, field, weights)
    *sends, kept = blur("final", tissue, gives, base, field, weights)
    arrived = [
        lax.ppermute(send, "owner", [(e[0], e[1]) for e in step])
        for send, step in zip(sends, SENDS)
    ]
    return store_call(takes, arrived + [kept])


def solution(mesh):
    in_specs = (P("slab", "owner", None), P("slab", "owner"), P())
    out_specs = P(("slab", "owner"), None, None, None)
    return jax.shard_map(body, mesh=mesh, in_specs=in_specs, out_specs=out_specs, check_vma=False)
```

```python
import jax
import jax.numpy as jnp
import numpy as np
from jax import lax
from jax.experimental import pallas as pl
from jax.experimental.pallas import tpu as pltpu
from jax.sharding import PartitionSpec as P

ITERS = 2
ratio_floor = 0.05

BX, BY, BZ = 64, 128, 128
TAPS, HALF = 33, 16
EDGE = 32
TILES = 8
CAP = 7
OWNERS = 16
MID = BY - 2 * HALF
WIDE = 12

bf16 = jnp.bfloat16
f32 = jnp.float32
VM = pl.BlockSpec(memory_space=pltpu.VMEM)
SM = pl.BlockSpec(memory_space=pltpu.SMEM)
PARAMS = pltpu.CompilerParams(vmem_limit_bytes=14 << 20)


GROUP = (("e", 0), ("m", 0), ("m", 16), ("e", 16))


def first_rank(c):
    return 7 * c if c % 2 == 0 else 7 * (c - 1) + 8


def tile_edges():
    out = []
    for c in range(OWNERS):
        for k in range(8 if c % 2 == 0 else 6):
            rank = first_rank(c) + k
            out.append((c, rank % OWNERS, k, rank // OWNERS))
    return out


ROUTES = (
    (6, 11, 0, 9, 2, 7, 12, 5, 14, 3, 8, 1, 10, 15, 4, 13),
    (7, 9, 4, 10, 14, 8, 13, 3, 11, 1, 12, 2, 6, 0, 5, -1),
    (2, 8, 1, 11, 15, 9, 0, 6, 10, 4, 13, 3, 5, 14, 7, 12),
    (3, 12, 5, 6, 13, -1, 11, 2, 15, 0, 7, 14, 9, 1, 8, 10),
    (5, 10, 15, 8, 3, 4, 1, -1, 13, 2, 11, 0, 7, 12, 9, 14),
    (4, -1, 14, -1, 1, 6, 15, -1, 12, 5, 9, -1, 8, -1, 3, 11),
    (1, 13, 3, 7, 0, -1, 10, 4, 9, -1, 6, 15, 11, -1, 2, -1),
    (-1, -1, -1, -1, 12, -1, 14, -1, -1, -1, -1, -1, 4, -1, 6, -1),
)
EDGES = tile_edges()
SENDS = [[e for e in EDGES if e[0] != e[1] and to[e[0]] == e[1]] for to in ROUTES]
NSEND = len(SENDS)
assert sum(map(len, SENDS)) + sum(e[0] == e[1] for e in EDGES) == len(EDGES)
GIVES = [[0] * (NSEND + 1) for _ in range(OWNERS)]
TAKES = [[-1] * (NSEND + 1) for _ in range(OWNERS)]
for _c, _step in enumerate(SENDS + [[e for e in EDGES if e[0] == e[1]]]):
    for _e in _step:
        GIVES[_e[0]][_c] = _e[2]
        TAKES[_e[1]][_c] = _e[3]


def parts(values):
    high = values.astype(bf16)
    return high, (values - high.astype(f32)).astype(bf16)


def band(taps_ref, axis, distance, flip):
    total = taps_ref[axis, 0]
    for k in range(1, TAPS):
        total = total + taps_ref[axis, k]
    acc = jnp.zeros(distance.shape, f32)
    for k in range(TAPS):
        tap = taps_ref[axis, TAPS - 1 - k if flip else k]
        acc = jnp.where(distance == k, tap, acc)
    return acc / total


def grid(rows, cols):
    return (
        lax.broadcasted_iota(jnp.int32, (rows, cols), 0),
        lax.broadcasted_iota(jnp.int32, (rows, cols), 1),
    )


def z_weights(taps_ref, flip, z_ref):
    r, c = grid(BZ, BZ)
    high, low = parts(band(taps_ref, 2, r - c + HALF, flip))
    z_ref[flip, 0:128, 0:128] = high
    z_ref[flip, 128:256, 0:128] = high
    z_ref[flip, 0:128, 128:256] = low
    z_ref[flip, 128:256, 128:256] = jnp.zeros((128, 128), bf16)


def weight_kernel(taps_ref, x_ref, y_ref, e_ref, z_ref):
    for flip in (0, 1):
        r, c = grid(128, 384)
        high, low = parts(band(taps_ref, 0, jnp.where((r % 8) == (c % 8), c // 8 - r // 8, -1), flip))
        x_ref[flip, :, 0:384] = high
        x_ref[flip, :, 384:768] = high
        x_ref[flip, :, 768:1152] = low
        r, c = grid(MID, BY)
        high, low = parts(band(taps_ref, 1, c - r, flip))
        y_ref[flip, :, 0:128] = high
        y_ref[flip, :, 128:256] = high
        y_ref[flip, :, 256:384] = low
        r, c = grid(64, 192)
        p = c - 48 * ((c >= 48).astype(jnp.int32) + (c >= 96) + (c >= 144))
        side = jnp.where(c >= 96, c - 96, c) >= 48
        same = ((r & 16) > 0) == side
        both = band(taps_ref, 1, jnp.where(same, p - (r & 15), -1), flip)
        high, low = parts(both)
        rest = jnp.where(c < 96, low.astype(f32), 0.0)
        e_ref[flip] = jnp.where(r < 32, high.astype(f32), rest).astype(bf16)
        z_weights(taps_ref, flip, z_ref)


def neighbours():
    row, me = lax.axis_index("slab"), lax.axis_index("owner")
    ends = [row > 0, row < lax.axis_size("slab") - 1, me > 0, me < lax.axis_size("owner") - 1]
    return [jnp.where(end, 1.0, 0.0).astype(f32) for end in ends]


def call(kernel, name, outs, scratch, small, arrays, micros=1.0):
    cost = pl.CostEstimate(
        flops=int(1.1e9 * micros), bytes_accessed=int(3.6e6 * micros), transcendentals=0
    )
    return pl.pallas_call(
        kernel,
        cost_estimate=cost,
        out_shape=tuple(outs),
        in_specs=[SM] * len(small) + [VM] * len(arrays),
        out_specs=(VM,) * len(outs),
        scratch_shapes=scratch,
        compiler_params=PARAMS,
        name=name,
    )(*small, *arrays)


def arr(*shape, dtype=f32):
    return jax.ShapeDtypeStruct(shape, dtype)


def make_weights(point_spread):
    outs = [
        arr(2, 128, 1152, dtype=bf16),
        arr(2, MID, 384, dtype=bf16),
        arr(2, 64, 192, dtype=bf16),
        arr(2, 256, 256, dtype=bf16),
    ]
    return call(weight_kernel, "weights", outs, [], [point_spread], [], 3.0)


def z_pass(rows, weights):
    high, low = parts(rows)
    both = jnp.dot(jnp.concatenate([high, low], axis=1), weights, preferred_element_type=f32)
    return both[:, :128] + both[:, 128:]


def keep(out, lines, row0, high_ref, low_ref):
    octets = out.shape[0] // 8
    out = jnp.concatenate(
        [out[:, 128 * i : 128 * i + 128].reshape(octets, 8, 128) for i in range(lines)], axis=1
    )
    high, low = parts(out)
    rows = pl.ds(pl.multiple_of(row0 * 8, 64), 8 * lines)
    high_ref[:, rows, :] = high
    low_ref[:, rows, :] = low


def y_mid(lines, weights, row0, high_ref, low_ref):
    high, low = parts(jnp.concatenate(lines, axis=1))
    out = jnp.dot(weights, jnp.concatenate([high, low, high], axis=0), preferred_element_type=f32)
    keep(out, len(lines), row0, high_ref, low_ref)


def y_edges(lines, weights, row0, high_ref, low_ref):
    high, low = parts(jnp.concatenate(lines, axis=1))
    out = jnp.dot(weights, jnp.concatenate([high, low], axis=0), preferred_element_type=f32)
    keep(out[:32] + out[32:], len(lines), row0, high_ref, low_ref)


def each_eight(rows, line, use):
    def step(i, carry):
        use([line(i * 8 + k) for k in range(8)], i * 8)
        return carry

    lax.fori_loop(0, rows // 8, step, 0, unroll=True)


def own_rows(make, use):
    each_eight(16, lambda r: make("e", r, r), lambda lines, r: use(lines, r))
    each_eight(32, lambda r: make("m", r, r + 16), lambda lines, r: use(lines, r + 16))
    each_eight(16, lambda r: make("e", r + 16, r + 48), lambda lines, r: use(lines, r + 48))


def x_dot(weights, high, low):
    return jnp.dot(
        weights, jnp.concatenate([high, low, high], axis=0), preferred_element_type=f32
    )


def split_lanes(out, count):
    return [out[:, 128 * i : 128 * i + 128] for i in range(count)]


def get(ref, row, octet):
    col = octet * 8 if isinstance(octet, int) else pl.multiple_of(octet * 8, 8)
    return ref[row : row + 16, pl.ds(col, 8), :].reshape(128, 128)


def put(ref, row, octet, piece):
    col = octet * 8 if isinstance(octet, int) else pl.multiple_of(octet * 8, 8)
    ref[row : row + 16, pl.ds(col, 8), :] = piece.reshape(16, 8, 128)


def masked_piece(observed, tissue, g, octet):
    return get(observed, 16 * g, octet) * tissue[g // 2, octet // 4].astype(f32)


def finish(kind, z_ref, pieces, bases):
    if kind == "ratio":
        return [[base / jnp.maximum(p, ratio_floor) for p, base in zip(pieces, bases)]]
    factor = z_pass(jnp.concatenate(pieces, axis=0), z_ref[1])
    new = jnp.concatenate(bases, axis=0) * factor
    fields = [new] if kind == "final" else [new, z_pass(new, z_ref[0])]
    return [
        [field[128 * i : 128 * i + 128] for i in range(len(pieces))] for field in fields
    ]


def count_out(kind):
    return 2 if kind == "update" else 1


def flip_of(kind):
    return 0 if kind == "ratio" else 1


def mid_finish(kind, tissue, base, z_ref, outs, g, o0, pieces):
    row = GROUP[g][1]
    bases = [
        get(base, row, o0 + i)
        if kind == "final"
        else masked_piece(base, tissue, g, o0 + i + 2)
        for i in range(WIDE)
    ]
    for ref, field in zip(outs, finish(kind, z_ref, pieces, bases)):
        for i in range(WIDE):
            put(ref, row, o0 + i, field[i])


EDGE_OCTETS = (0, 1, 14, 15)


def edge_finish(kind, tissue, base, z_ref, outs, groups, pieces):
    places = [(g, i) for g in groups for i in range(4)]
    bases = [
        get(base[i // 2], GROUP[g][1], i % 2)
        if kind == "final"
        else masked_piece(base[0], tissue, g, EDGE_OCTETS[i])
        for g, i in places
    ]
    for refs, field in zip(outs, finish(kind, z_ref, pieces, bases)):
        for (g, i), piece in zip(places, field):
            put(refs[i // 2], GROUP[g][1], i % 2, piece)


def kernel_a(kind):
    def run(tissue, base, lo_m, lo_e, mid_m, mid_e, hi_m, hi_e, x_ref, y_ref, z_ref, *outs):
        outs, (high_ref, low_ref) = outs[:-2], outs[-2:]
        flip = flip_of(kind)
        own = {"m": (lo_m, mid_m, hi_m), "e": (lo_e, mid_e, hi_e)}
        own_rows(
            lambda part, r, x: jnp.concatenate([ref[r] for ref in own[part]], axis=0),
            lambda lines, x: y_mid(lines, y_ref[flip], x, high_ref, low_ref),
        )

        def step(q, carry):
            o0 = q * WIDE
            for g in (1, 2):
                rows = slice(128 * (g - 1), 128 * (g - 1) + 384)
                high = jnp.concatenate([high_ref[o0 + i, rows] for i in range(WIDE)], axis=1)
                low = jnp.concatenate([low_ref[o0 + i, rows] for i in range(WIDE)], axis=1)
                pieces = split_lanes(x_dot(x_ref[flip], high, low), WIDE)
                mid_finish(kind, tissue, base, z_ref, outs, g, o0, pieces)
            return carry

        lax.fori_loop(0, MID // 8 // WIDE, step, 0, unroll=True)

    return run


def kernel_b(kind):
    def run(tissue, base, xm, xp, own_high, own_low, x_ref, y_ref, z_ref, *outs):
        outs, (high_ref, low_ref) = outs[:-2], outs[-2:]
        flip, inside = flip_of(kind), neighbours()
        for halo, near, row0 in ((xm, inside[0], 0), (xp, inside[1], 16)):
            each_eight(
                16,
                lambda r, halo=halo, near=near: halo[r] * near,
                lambda lines, r, row0=row0: y_mid(
                    lines, y_ref[flip], r + row0, high_ref, low_ref
                ),
            )

        def step(q, carry):
            o0 = q * WIDE
            for g in (0, 3):

                def rows(halo_ref, own_ref):
                    if g == 0:
                        both = [
                            jnp.concatenate(
                                [halo_ref[o0 + i, 0:128], own_ref[o0 + i, 0:256]], axis=0
                            )
                            for i in range(WIDE)
                        ]
                    else:
                        both = [
                            jnp.concatenate(
                                [own_ref[o0 + i, 256:512], halo_ref[o0 + i, 128:256]], axis=0
                            )
                            for i in range(WIDE)
                        ]
                    return jnp.concatenate(both, axis=1)

                out = x_dot(x_ref[flip], rows(high_ref, own_high), rows(low_ref, own_low))
                mid_finish(kind, tissue, base, z_ref, outs, g, o0, split_lanes(out, WIDE))
            return carry

        lax.fori_loop(0, MID // 8 // WIDE, step, 0, unroll=True)

    return run


def kernel_c(kind):
    def run(tissue, *refs):
        nbase = 2 if kind == "final" else 1
        base, refs = refs[:nbase], refs[nbase:]
        (ym, yp, lo_m, lo_e, mid_m, mid_e, hi_m, hi_e), refs = refs[:8], refs[8:]
        (x_ref, e_ref, z_ref), refs = refs[:3], refs[3:]
        outs, (high_ref, low_ref) = refs[:-2], refs[-2:]
        flip, inside = flip_of(kind), neighbours()
        own = {"m": (lo_m, mid_m, hi_m), "e": (lo_e, mid_e, hi_e)}

        def line(part, r, x):
            lo, mid, hi = own[part]
            return jnp.concatenate(
                [
                    ym[x] * inside[2],
                    lo[r],
                    mid[r, :HALF],
                    mid[r, MID - HALF :],
                    hi[r],
                    yp[x] * inside[3],
                ],
                axis=0,
            )

        own_rows(line, lambda lines, x: y_edges(lines, e_ref[flip], x, high_ref, low_ref))
        pieces = []
        for g in (1, 2):
            rows = slice(128 * (g - 1), 128 * (g - 1) + 384)
            high = jnp.concatenate([high_ref[i, rows] for i in range(4)], axis=1)
            low = jnp.concatenate([low_ref[i, rows] for i in range(4)], axis=1)
            pieces += split_lanes(x_dot(x_ref[flip], high, low), 4)
        pairs = [outs[2 * f : 2 * f + 2] for f in range(count_out(kind))]
        edge_finish(kind, tissue, base, z_ref, pairs, (1, 2), pieces)

    return run


def edge_d(kind, tissue, base, xm, xp, cm, cp, own_high, own_low, x_ref, e_ref, z_ref, pairs, high_ref, low_ref):
    flip, inside = flip_of(kind), neighbours()
    for halo, corner, near, row0 in ((xm, cm, inside[0], 0), (xp, cp, inside[1], 16)):

        def line(r, halo=halo, corner=corner, near=near):
            return jnp.concatenate(
                [
                    corner[r, :HALF] * (near * inside[2]),
                    halo[r, : 2 * HALF] * near,
                    halo[r, BY - 2 * HALF :] * near,
                    corner[r, HALF:] * (near * inside[3]),
                ],
                axis=0,
            )

        each_eight(
            16,
            line,
            lambda lines, r, row0=row0: y_edges(lines, e_ref[flip], r + row0, high_ref, low_ref),
        )
    pieces = []
    for g in (0, 3):

        def rows(halo_ref, own_ref):
            if g == 0:
                both = [
                    jnp.concatenate([halo_ref[i, 0:128], own_ref[i, 0:256]], axis=0)
                    for i in range(4)
                ]
            else:
                both = [
                    jnp.concatenate([own_ref[i, 256:512], halo_ref[i, 128:256]], axis=0)
                    for i in range(4)
                ]
            return jnp.concatenate(both, axis=1)

        out = x_dot(x_ref[flip], rows(high_ref, own_high), rows(low_ref, own_low))
        pieces += split_lanes(out, 4)
    edge_finish(kind, tissue, base, z_ref, pairs, (0, 3), pieces)


def fill_strips(mid_e, lo_e, hi_e, lo_m, hi_m, xs_lo, xs_hi, ys_lo, ys_hi):
    for ref, ends, middle in ((ys_lo, lo_e, lo_m), (ys_hi, hi_e, hi_m)):
        ref[:16] = ends[:16]
        ref[16:48] = middle[...]
        ref[48:] = ends[16:]
    for ref, row in ((xs_lo, 0), (xs_hi, 16)):
        ref[:, :HALF, :] = lo_e[row : row + 16]
        ref[:, HALF : BY - HALF, :] = mid_e[row : row + 16]
        ref[:, BY - HALF :, :] = hi_e[row : row + 16]


def kernel_d(kind):
    def run(tissue, base, xm, xp, cm, cp, own_high, own_low, mid_e, lo_m, hi_m, x_ref, e_ref, z_ref, *outs):
        outs, edges, (high_ref, low_ref) = outs[:-6], outs[-6:-2], outs[-2:]
        pairs = [outs[2 * f : 2 * f + 2] for f in range(count_out(kind))]
        edge_d(
            kind, tissue, (base,), xm, xp, cm, cp, own_high, own_low,
            x_ref, e_ref, z_ref, pairs, high_ref, low_ref,
        )
        fill_strips(mid_e, *pairs[-1], lo_m, hi_m, *edges)

    return run


def kernel_last(tissue, gives, base_lo, base_hi, xm, xp, cm, cp, own_high, own_low, mid_m, mid_e, lo_m, hi_m, x_ref, e_ref, z_ref, *refs):
    sends, (lo_e, hi_e, high_ref, low_ref, tiles, nth) = refs[: NSEND + 1], refs[NSEND + 1 :]
    for t in range(TILES):
        nth[t] = 0
    count = jnp.int32(0)
    for t in range(TILES):
        flag = tissue[t // 4, t % 4]

        @pl.when(flag > 0)
        def _(t=t, count=count):
            nth[count] = t

        count = count + (flag > 0).astype(jnp.int32)
    edge_d(
        "final", tissue, (base_lo, base_hi), xm, xp, cm, cp, own_high, own_low,
        x_ref, e_ref, z_ref, [(lo_e, hi_e)], high_ref, low_ref,
    )
    for i in range(2):
        for (lo, mid, hi), row, half in (
            ((lo_e, mid_e, hi_e), 16 * i, 16 * i),
            ((lo_m, mid_m, hi_m), 16 * i, 16 * (1 - i)),
        ):
            rows, into = slice(row, row + 16), slice(half, half + 16)
            tiles[4 * i, into, :HALF] = lo[rows]
            tiles[4 * i, into, HALF:] = mid[rows, :HALF]
            tiles[4 * i + 1, into] = mid[rows, HALF : HALF + EDGE]
            tiles[4 * i + 2, into] = mid[rows, HALF + EDGE : HALF + 2 * EDGE]
            tiles[4 * i + 3, into, :HALF] = mid[rows, MID - HALF :]
            tiles[4 * i + 3, into, HALF:] = hi[rows]
    for c, send in enumerate(sends):
        send[...] = tiles[nth[gives[lax.axis_index("owner"), c]]]


def first_kernel(taps_ref, tissue, observed, lo_m, lo_e, mid_m, mid_e, hi_m, hi_e, *strips):
    strips, z_ref = strips[:-1], strips[-1]
    z_weights(taps_ref, 0, z_ref)
    mids, edges = {"m": mid_m, "e": mid_e}, {"m": (lo_m, hi_m), "e": (lo_e, hi_e)}
    for g, (part, row) in enumerate(GROUP):

        def step(q, carry, g=g, part=part, row=row):
            o0 = q * WIDE
            pieces = [masked_piece(observed, tissue, g, o0 + i + 2) for i in range(WIDE)]
            done = z_pass(jnp.concatenate(pieces, axis=0), z_ref[0])
            for i in range(WIDE):
                put(mids[part], row, o0 + i, done[128 * i : 128 * i + 128])
            return carry

        lax.fori_loop(0, MID // 8 // WIDE, step, 0, unroll=True)
        pieces = [masked_piece(observed, tissue, g, o) for o in EDGE_OCTETS]
        done = z_pass(jnp.concatenate(pieces, axis=0), z_ref[0])
        for i in range(4):
            put(edges[part][i // 2], row, i % 2, done[128 * i : 128 * i + 128])
    fill_strips(mid_e, lo_e, hi_e, lo_m, hi_m, *strips)


EDGE_PART = arr(32, HALF, BZ)
MID_PART = arr(32, MID, BZ)
STRIPS = [arr(HALF, BY, BZ)] * 2 + [arr(BX, HALF, BZ)] * 2
TILE_ARR = arr(EDGE, EDGE, BZ)


def own_parts(octets):
    return [arr(octets, 8 * BX, 128, dtype=bf16)] * 2


def halo_parts(octets):
    return [pltpu.VMEM((octets, 8 * 2 * HALF, 128), bf16)] * 2


def blur(kind, tissue, gives, base, field, weights):
    lo_m, lo_e, mid_m, mid_e, hi_m, hi_e, xs_lo, xs_hi, ys_lo, ys_hi = field
    wx, wy, we, wz = weights
    count = count_out(kind)
    ym = shift(ys_hi, "owner", 1)
    yp = shift(ys_lo, "owner", -1)
    xm = shift(xs_hi, "slab", 1)
    xp = shift(xs_lo, "slab", -1)
    if kind == "final":
        base_lo_m, base_lo_e, base_mid_m, base_mid_e, base_hi_m, base_hi_e = base
        base_c, base_d = [base_lo_m, base_hi_m], [base_lo_e, base_hi_e]
    else:
        base_mid_m = base_mid_e = base
        base_c = base_d = [base]
    own = [lo_m, lo_e, mid_m, mid_e, hi_m, hi_e]
    *new_mid_m, high, low = call(
        kernel_a(kind), kind + "_a", [MID_PART] * count + own_parts(MID // 8), [],
        [tissue], [base_mid_m, *own, wx, wy, wz], 4.0,
    )
    cm = shift(jnp.concatenate([ym[BX - HALF :], yp[BX - HALF :]], axis=1), "slab", 1)
    cp = shift(jnp.concatenate([ym[:HALF], yp[:HALF]], axis=1), "slab", -1)
    new_mid_e = call(
        kernel_b(kind), kind + "_b", [MID_PART] * count, halo_parts(MID // 8),
        [tissue], [base_mid_e, xm, xp, high, low, wx, wy, wz], 3.0,
    )
    *new_m, edge_high, edge_low = call(
        kernel_c(kind), kind + "_c", [EDGE_PART] * (2 * count) + own_parts(4), [],
        [tissue], [*base_c, ym, yp, *own, wx, we, wz], 2.0,
    )
    late = [xm, xp, cm, cp, edge_high, edge_low]
    if kind == "final":
        scratch = [pltpu.VMEM((32, HALF, BZ), f32)] * 2 + halo_parts(4)
        scratch += [pltpu.VMEM((TILES, EDGE, EDGE, BZ), f32), pltpu.SMEM((TILES,), jnp.int32)]
        return call(
            kernel_last, "final_d", [TILE_ARR] * (NSEND + 1), scratch,
            [tissue, gives],
            [*base_d, *late, new_mid_m[0], new_mid_e[0], *new_m, wx, we, wz], 2.0,
        )
    *new_e, xs_lo, xs_hi, ys_lo, ys_hi = call(
        kernel_d(kind), kind + "_d", [EDGE_PART] * (2 * count) + STRIPS, halo_parts(4),
        [tissue], [*base_d, *late, new_mid_e[-1], *new_m[-2:], wx, we, wz], 2.0,
    )
    fields = [
        [
            new_m[2 * f], new_e[2 * f], new_mid_m[f], new_mid_e[f], new_m[2 * f + 1],
            new_e[2 * f + 1],
        ]
        for f in range(count)
    ]
    return fields[:-1] + [fields[-1] + [xs_lo, xs_hi, ys_lo, ys_hi]]


def store_kernel(first, count):
    def run(takes, *refs):
        arrived, out, sems = refs[:count], refs[-2], refs[-1]
        me = lax.axis_index("owner")

        def copy(c):
            slot = jnp.maximum(takes[me, first + c], 0)
            return pltpu.make_async_copy(arrived[c], out.at[slot], sems.at[c])

        for c in range(count):

            @pl.when(takes[me, first + c] >= 0)
            def _(c=c):
                copy(c).start()

        for c in range(count):

            @pl.when(takes[me, first + c] >= 0)
            def _(c=c):
                copy(c).wait()

    return run


def store_call(takes, first, arrived, packed=None):
    any_spec = pl.BlockSpec(memory_space=pl.ANY)
    count = len(arrived)
    arrays = list(arrived) + ([] if packed is None else [packed])
    return pl.pallas_call(
        store_kernel(first, count),
        out_shape=jax.ShapeDtypeStruct((CAP, EDGE, EDGE, BZ), f32),
        in_specs=[SM] + [any_spec] * len(arrays),
        out_specs=any_spec,
        scratch_shapes=[pltpu.SemaphoreType.DMA((count,))],
        input_output_aliases={} if packed is None else {len(arrays): 0},
        compiler_params=PARAMS,
        name="store",
    )(takes, *arrays)


def shift(values, axis, step):
    count = lax.axis_size(axis)
    return lax.ppermute(values, axis, [(i, (i + step) % count) for i in range(count)])


def body(observed, tissue, point_spread):
    weights = make_weights(point_spread)
    gives = jnp.asarray(GIVES, jnp.int32)
    takes = np.asarray(TAKES, np.int32)
    outs = [EDGE_PART] * 2 + [MID_PART] * 2 + [EDGE_PART] * 2 + STRIPS
    scratch = [pltpu.VMEM((1, 256, 256), bf16)]
    field = call(first_kernel, "first", outs, scratch, [point_spread, tissue], [observed], 2.0)
    base = observed
    for iteration in range(ITERS):
        (field,) = blur("ratio", tissue, gives, observed, field, weights)
        if iteration < ITERS - 1:
            base, field = blur("update", tissue, gives, base, field, weights)
    *sends, kept = blur("final", tissue, gives, base, field, weights)
    arrived = [
        lax.ppermute(send, "owner", [(e[0], e[1]) for e in step])
        for send, step in zip(sends, SENDS)
    ]
    last = NSEND - 2
    packed = store_call(takes[:, list(range(last)) + [NSEND]], 0, arrived[:last] + [kept])
    return store_call(takes[:, last:NSEND], 0, arrived[last:], packed)


def solution(mesh):
    in_specs = (P("slab", "owner", None), P("slab", "owner"), P())
    out_specs = P(("slab", "owner"), None, None, None)
    return jax.shard_map(body, mesh=mesh, in_specs=in_specs, out_specs=out_specs, check_vma=False)
```

```python
import jax
import jax.numpy as jnp
import numpy as np
from jax import lax
from jax.experimental import pallas as pl
from jax.experimental.pallas import tpu as pltpu
from jax.sharding import PartitionSpec as P

ITERS = 2
ratio_floor = 0.05

BX, BY, BZ = 64, 128, 128
TAPS, HALF = 33, 16
EDGE = 32
TILES = 8
CAP = 7
OWNERS = 16
MID = BY - 2 * HALF
WIDE = 12

bf16 = jnp.bfloat16
f32 = jnp.float32
VM = pl.BlockSpec(memory_space=pltpu.VMEM)
SM = pl.BlockSpec(memory_space=pltpu.SMEM)
PARAMS = pltpu.CompilerParams(vmem_limit_bytes=14 << 20)


GROUP = (("e", 0), ("m", 0), ("m", 16), ("e", 16))


def first_rank(c):
    return 7 * c if c % 2 == 0 else 7 * (c - 1) + 8


def tile_edges():
    out = []
    for c in range(OWNERS):
        for k in range(8 if c % 2 == 0 else 6):
            rank = first_rank(c) + k
            out.append((c, rank % OWNERS, k, rank // OWNERS))
    return out


ROUTES = (
    (6, 11, 0, 9, 2, 7, 12, 5, 14, 3, 8, 1, 10, 15, 4, 13),
    (2, 8, 1, 11, 15, 9, 0, 6, 10, 4, 13, 3, 5, 14, 7, 12),
    (7, 9, 4, 10, 14, 8, 13, 3, 11, 1, 12, 2, 6, 0, 5, -1),
    (3, 12, 5, 6, 13, -1, 11, 2, 15, 0, 7, 14, 9, 1, 8, 10),
    (4, -1, 14, -1, 1, 6, 15, -1, 12, 5, 9, -1, 8, -1, 3, 11),
    (5, 10, 15, 8, 3, 4, 1, -1, 13, 2, 11, 0, 7, 12, 9, 14),
    (1, 13, 3, 7, 0, -1, 10, 4, 9, -1, 6, 15, 11, -1, 2, -1),
    (-1, -1, -1, -1, 12, -1, 14, -1, -1, -1, -1, -1, 4, -1, 6, -1),
)
EDGES = tile_edges()
SENDS = [[e for e in EDGES if e[0] != e[1] and to[e[0]] == e[1]] for to in ROUTES]
NSEND = len(SENDS)
assert sum(map(len, SENDS)) + sum(e[0] == e[1] for e in EDGES) == len(EDGES)
GIVES = [[0] * (NSEND + 1) for _ in range(OWNERS)]
TAKES = [[-1] * (NSEND + 1) for _ in range(OWNERS)]
for _c, _step in enumerate(SENDS + [[e for e in EDGES if e[0] == e[1]]]):
    for _e in _step:
        GIVES[_e[0]][_c] = _e[2]
        TAKES[_e[1]][_c] = _e[3]


def parts(values):
    high = values.astype(bf16)
    return high, (values - high.astype(f32)).astype(bf16)


def band(taps_ref, axis, distance, flip):
    total = taps_ref[axis, 0]
    for k in range(1, TAPS):
        total = total + taps_ref[axis, k]
    acc = jnp.zeros(distance.shape, f32)
    for k in range(TAPS):
        tap = taps_ref[axis, TAPS - 1 - k if flip else k]
        acc = jnp.where(distance == k, tap, acc)
    return acc / total


def grid(rows, cols):
    return (
        lax.broadcasted_iota(jnp.int32, (rows, cols), 0),
        lax.broadcasted_iota(jnp.int32, (rows, cols), 1),
    )


def z_weights(taps_ref, flip, z_ref):
    r, c = grid(BZ, BZ)
    high, low = parts(band(taps_ref, 2, r - c + HALF, flip))
    z_ref[flip, 0:128, 0:128] = high
    z_ref[flip, 128:256, 0:128] = high
    z_ref[flip, 0:128, 128:256] = low
    z_ref[flip, 128:256, 128:256] = jnp.zeros((128, 128), bf16)


def weight_kernel(taps_ref, x_ref, y_ref, e_ref, z_ref):
    for flip in (0, 1):
        r, c = grid(128, 384)
        high, low = parts(band(taps_ref, 0, jnp.where((r % 8) == (c % 8), c // 8 - r // 8, -1), flip))
        x_ref[flip, :, 0:384] = high
        x_ref[flip, :, 384:768] = high
        x_ref[flip, :, 768:1152] = low
        r, c = grid(MID, BY)
        high, low = parts(band(taps_ref, 1, c - r, flip))
        y_ref[flip, :, 0:128] = high
        y_ref[flip, :, 128:256] = high
        y_ref[flip, :, 256:384] = low
        r, c = grid(64, 192)
        p = c - 48 * ((c >= 48).astype(jnp.int32) + (c >= 96) + (c >= 144))
        side = jnp.where(c >= 96, c - 96, c) >= 48
        same = ((r & 16) > 0) == side
        both = band(taps_ref, 1, jnp.where(same, p - (r & 15), -1), flip)
        high, low = parts(both)
        rest = jnp.where(c < 96, low.astype(f32), 0.0)
        e_ref[flip] = jnp.where(r < 32, high.astype(f32), rest).astype(bf16)
        z_weights(taps_ref, flip, z_ref)


def neighbours():
    row, me = lax.axis_index("slab"), lax.axis_index("owner")
    ends = [row > 0, row < lax.axis_size("slab") - 1, me > 0, me < lax.axis_size("owner") - 1]
    return [jnp.where(end, 1.0, 0.0).astype(f32) for end in ends]


def call(kernel, name, outs, scratch, small, arrays, micros=1.0):
    cost = pl.CostEstimate(
        flops=int(1.1e9 * micros), bytes_accessed=int(3.6e6 * micros), transcendentals=0
    )
    return pl.pallas_call(
        kernel,
        cost_estimate=cost,
        out_shape=tuple(outs),
        in_specs=[SM] * len(small) + [VM] * len(arrays),
        out_specs=(VM,) * len(outs),
        scratch_shapes=scratch,
        compiler_params=PARAMS,
        name=name,
    )(*small, *arrays)


def arr(*shape, dtype=f32):
    return jax.ShapeDtypeStruct(shape, dtype)


def make_weights(point_spread):
    outs = [
        arr(2, 128, 1152, dtype=bf16),
        arr(2, MID, 384, dtype=bf16),
        arr(2, 64, 192, dtype=bf16),
        arr(2, 256, 256, dtype=bf16),
    ]
    return call(weight_kernel, "weights", outs, [], [point_spread], [], 3.0)


def z_pass(rows, weights):
    high, low = parts(rows)
    both = jnp.dot(jnp.concatenate([high, low], axis=1), weights, preferred_element_type=f32)
    return both[:, :128] + both[:, 128:]


def keep(out, lines, row0, high_ref, low_ref):
    octets = out.shape[0] // 8
    out = jnp.concatenate(
        [out[:, 128 * i : 128 * i + 128].reshape(octets, 8, 128) for i in range(lines)], axis=1
    )
    high, low = parts(out)
    rows = pl.ds(pl.multiple_of(row0 * 8, 64), 8 * lines)
    high_ref[:, rows, :] = high
    low_ref[:, rows, :] = low


def y_mid(lines, weights, row0, high_ref, low_ref):
    high, low = parts(jnp.concatenate(lines, axis=1))
    out = jnp.dot(weights, jnp.concatenate([high, low, high], axis=0), preferred_element_type=f32)
    keep(out, len(lines), row0, high_ref, low_ref)


def y_edges(lines, weights, row0, high_ref, low_ref):
    high, low = parts(jnp.concatenate(lines, axis=1))
    out = jnp.dot(weights, jnp.concatenate([high, low], axis=0), preferred_element_type=f32)
    keep(out[:32] + out[32:], len(lines), row0, high_ref, low_ref)


def each_eight(rows, line, use):
    def step(i, carry):
        use([line(i * 8 + k) for k in range(8)], i * 8)
        return carry

    lax.fori_loop(0, rows // 8, step, 0, unroll=True)


def own_rows(make, use):
    each_eight(16, lambda r: make("e", r, r), lambda lines, r: use(lines, r))
    each_eight(32, lambda r: make("m", r, r + 16), lambda lines, r: use(lines, r + 16))
    each_eight(16, lambda r: make("e", r + 16, r + 48), lambda lines, r: use(lines, r + 48))


def x_dot(weights, high, low):
    return jnp.dot(
        weights, jnp.concatenate([high, low, high], axis=0), preferred_element_type=f32
    )


def split_lanes(out, count):
    return [out[:, 128 * i : 128 * i + 128] for i in range(count)]


def get(ref, row, octet):
    col = octet * 8 if isinstance(octet, int) else pl.multiple_of(octet * 8, 8)
    return ref[row : row + 16, pl.ds(col, 8), :].reshape(128, 128)


def put(ref, row, octet, piece):
    col = octet * 8 if isinstance(octet, int) else pl.multiple_of(octet * 8, 8)
    ref[row : row + 16, pl.ds(col, 8), :] = piece.reshape(16, 8, 128)


def masked_piece(observed, tissue, g, octet):
    return get(observed, 16 * g, octet) * tissue[g // 2, octet // 4].astype(f32)


def finish(kind, z_ref, pieces, bases):
    if kind == "ratio":
        return [[base / jnp.maximum(p, ratio_floor) for p, base in zip(pieces, bases)]]
    factor = z_pass(jnp.concatenate(pieces, axis=0), z_ref[1])
    new = jnp.concatenate(bases, axis=0) * factor
    fields = [new] if kind == "final" else [new, z_pass(new, z_ref[0])]
    return [
        [field[128 * i : 128 * i + 128] for i in range(len(pieces))] for field in fields
    ]


def count_out(kind):
    return 2 if kind == "update" else 1


def flip_of(kind):
    return 0 if kind == "ratio" else 1


def mid_finish(kind, tissue, base, z_ref, outs, g, o0, pieces):
    row = GROUP[g][1]
    bases = [
        get(base, row, o0 + i)
        if kind == "final"
        else masked_piece(base, tissue, g, o0 + i + 2)
        for i in range(WIDE)
    ]
    for ref, field in zip(outs, finish(kind, z_ref, pieces, bases)):
        for i in range(WIDE):
            put(ref, row, o0 + i, field[i])


EDGE_OCTETS = (0, 1, 14, 15)


def edge_finish(kind, tissue, base, z_ref, outs, groups, pieces):
    places = [(g, i) for g in groups for i in range(4)]
    bases = [
        get(base[i // 2], GROUP[g][1], i % 2)
        if kind == "final"
        else masked_piece(base[0], tissue, g, EDGE_OCTETS[i])
        for g, i in places
    ]
    for refs, field in zip(outs, finish(kind, z_ref, pieces, bases)):
        for (g, i), piece in zip(places, field):
            put(refs[i // 2], GROUP[g][1], i % 2, piece)


def kernel_a(kind):
    def run(tissue, base, lo_m, lo_e, mid_m, mid_e, hi_m, hi_e, x_ref, y_ref, z_ref, *outs):
        outs, (high_ref, low_ref) = outs[:-2], outs[-2:]
        flip = flip_of(kind)
        own = {"m": (lo_m, mid_m, hi_m), "e": (lo_e, mid_e, hi_e)}
        own_rows(
            lambda part, r, x: jnp.concatenate([ref[r] for ref in own[part]], axis=0),
            lambda lines, x: y_mid(lines, y_ref[flip], x, high_ref, low_ref),
        )

        def step(q, carry):
            o0 = q * WIDE
            for g in (1, 2):
                rows = slice(128 * (g - 1), 128 * (g - 1) + 384)
                high = jnp.concatenate([high_ref[o0 + i, rows] for i in range(WIDE)], axis=1)
                low = jnp.concatenate([low_ref[o0 + i, rows] for i in range(WIDE)], axis=1)
                pieces = split_lanes(x_dot(x_ref[flip], high, low), WIDE)
                mid_finish(kind, tissue, base, z_ref, outs, g, o0, pieces)
            return carry

        lax.fori_loop(0, MID // 8 // WIDE, step, 0, unroll=True)

    return run


def kernel_b(kind):
    def run(tissue, base, xm, xp, own_high, own_low, x_ref, y_ref, z_ref, *outs):
        outs, (high_ref, low_ref) = outs[:-2], outs[-2:]
        flip, inside = flip_of(kind), neighbours()
        for halo, near, row0 in ((xm, inside[0], 0), (xp, inside[1], 16)):
            each_eight(
                16,
                lambda r, halo=halo, near=near: halo[r] * near,
                lambda lines, r, row0=row0: y_mid(
                    lines, y_ref[flip], r + row0, high_ref, low_ref
                ),
            )

        def step(q, carry):
            o0 = q * WIDE
            for g in (0, 3):

                def rows(halo_ref, own_ref):
                    if g == 0:
                        both = [
                            jnp.concatenate(
                                [halo_ref[o0 + i, 0:128], own_ref[o0 + i, 0:256]], axis=0
                            )
                            for i in range(WIDE)
                        ]
                    else:
                        both = [
                            jnp.concatenate(
                                [own_ref[o0 + i, 256:512], halo_ref[o0 + i, 128:256]], axis=0
                            )
                            for i in range(WIDE)
                        ]
                    return jnp.concatenate(both, axis=1)

                out = x_dot(x_ref[flip], rows(high_ref, own_high), rows(low_ref, own_low))
                mid_finish(kind, tissue, base, z_ref, outs, g, o0, split_lanes(out, WIDE))
            return carry

        lax.fori_loop(0, MID // 8 // WIDE, step, 0, unroll=True)

    return run


def kernel_c(kind):
    def run(tissue, *refs):
        nbase = 2 if kind == "final" else 1
        base, refs = refs[:nbase], refs[nbase:]
        (ym, yp, lo_m, lo_e, mid_m, mid_e, hi_m, hi_e), refs = refs[:8], refs[8:]
        (x_ref, e_ref, z_ref), refs = refs[:3], refs[3:]
        outs, (high_ref, low_ref) = refs[:-2], refs[-2:]
        flip, inside = flip_of(kind), neighbours()
        own = {"m": (lo_m, mid_m, hi_m), "e": (lo_e, mid_e, hi_e)}

        def line(part, r, x):
            lo, mid, hi = own[part]
            return jnp.concatenate(
                [
                    ym[x] * inside[2],
                    lo[r],
                    mid[r, :HALF],
                    mid[r, MID - HALF :],
                    hi[r],
                    yp[x] * inside[3],
                ],
                axis=0,
            )

        own_rows(line, lambda lines, x: y_edges(lines, e_ref[flip], x, high_ref, low_ref))
        pieces = []
        for g in (1, 2):
            rows = slice(128 * (g - 1), 128 * (g - 1) + 384)
            high = jnp.concatenate([high_ref[i, rows] for i in range(4)], axis=1)
            low = jnp.concatenate([low_ref[i, rows] for i in range(4)], axis=1)
            pieces += split_lanes(x_dot(x_ref[flip], high, low), 4)
        pairs = [outs[2 * f : 2 * f + 2] for f in range(count_out(kind))]
        edge_finish(kind, tissue, base, z_ref, pairs, (1, 2), pieces)

    return run


def edge_d(kind, tissue, base, xm, xp, cm, cp, own_high, own_low, x_ref, e_ref, z_ref, pairs, high_ref, low_ref):
    flip, inside = flip_of(kind), neighbours()
    for halo, corner, near, row0 in ((xm, cm, inside[0], 0), (xp, cp, inside[1], 16)):

        def line(r, halo=halo, corner=corner, near=near):
            return jnp.concatenate(
                [
                    corner[r, :HALF] * (near * inside[2]),
                    halo[r, : 2 * HALF] * near,
                    halo[r, BY - 2 * HALF :] * near,
                    corner[r, HALF:] * (near * inside[3]),
                ],
                axis=0,
            )

        each_eight(
            16,
            line,
            lambda lines, r, row0=row0: y_edges(lines, e_ref[flip], r + row0, high_ref, low_ref),
        )
    pieces = []
    for g in (0, 3):

        def rows(halo_ref, own_ref):
            if g == 0:
                both = [
                    jnp.concatenate([halo_ref[i, 0:128], own_ref[i, 0:256]], axis=0)
                    for i in range(4)
                ]
            else:
                both = [
                    jnp.concatenate([own_ref[i, 256:512], halo_ref[i, 128:256]], axis=0)
                    for i in range(4)
                ]
            return jnp.concatenate(both, axis=1)

        out = x_dot(x_ref[flip], rows(high_ref, own_high), rows(low_ref, own_low))
        pieces += split_lanes(out, 4)
    edge_finish(kind, tissue, base, z_ref, pairs, (0, 3), pieces)


def fill_strips(mid_e, lo_e, hi_e, lo_m, hi_m, xs_lo, xs_hi, ys_lo, ys_hi):
    for ref, ends, middle in ((ys_lo, lo_e, lo_m), (ys_hi, hi_e, hi_m)):
        ref[:16] = ends[:16]
        ref[16:48] = middle[...]
        ref[48:] = ends[16:]
    for ref, row in ((xs_lo, 0), (xs_hi, 16)):
        ref[:, :HALF, :] = lo_e[row : row + 16]
        ref[:, HALF : BY - HALF, :] = mid_e[row : row + 16]
        ref[:, BY - HALF :, :] = hi_e[row : row + 16]


def kernel_d(kind):
    def run(tissue, base, xm, xp, cm, cp, own_high, own_low, mid_e, lo_m, hi_m, x_ref, e_ref, z_ref, *outs):
        outs, edges, (high_ref, low_ref) = outs[:-6], outs[-6:-2], outs[-2:]
        pairs = [outs[2 * f : 2 * f + 2] for f in range(count_out(kind))]
        edge_d(
            kind, tissue, (base,), xm, xp, cm, cp, own_high, own_low,
            x_ref, e_ref, z_ref, pairs, high_ref, low_ref,
        )
        fill_strips(mid_e, *pairs[-1], lo_m, hi_m, *edges)

    return run


def kernel_last(tissue, gives, base_lo, base_hi, xm, xp, cm, cp, own_high, own_low, mid_m, mid_e, lo_m, hi_m, x_ref, e_ref, z_ref, *refs):
    sends, (lo_e, hi_e, high_ref, low_ref, tiles, nth) = refs[: NSEND + 1], refs[NSEND + 1 :]
    for t in range(TILES):
        nth[t] = 0
    count = jnp.int32(0)
    for t in range(TILES):
        flag = tissue[t // 4, t % 4]

        @pl.when(flag > 0)
        def _(t=t, count=count):
            nth[count] = t

        count = count + (flag > 0).astype(jnp.int32)
    edge_d(
        "final", tissue, (base_lo, base_hi), xm, xp, cm, cp, own_high, own_low,
        x_ref, e_ref, z_ref, [(lo_e, hi_e)], high_ref, low_ref,
    )
    for i in range(2):
        for (lo, mid, hi), row, half in (
            ((lo_e, mid_e, hi_e), 16 * i, 16 * i),
            ((lo_m, mid_m, hi_m), 16 * i, 16 * (1 - i)),
        ):
            rows, into = slice(row, row + 16), slice(half, half + 16)
            tiles[4 * i, into, :HALF] = lo[rows]
            tiles[4 * i, into, HALF:] = mid[rows, :HALF]
            tiles[4 * i + 1, into] = mid[rows, HALF : HALF + EDGE]
            tiles[4 * i + 2, into] = mid[rows, HALF + EDGE : HALF + 2 * EDGE]
            tiles[4 * i + 3, into, :HALF] = mid[rows, MID - HALF :]
            tiles[4 * i + 3, into, HALF:] = hi[rows]
    for c, send in enumerate(sends):
        send[...] = tiles[nth[gives[lax.axis_index("owner"), c]]]


def first_kernel(taps_ref, tissue, observed, lo_m, lo_e, mid_m, mid_e, hi_m, hi_e, *strips):
    strips, z_ref = strips[:-1], strips[-1]
    z_weights(taps_ref, 0, z_ref)
    mids, edges = {"m": mid_m, "e": mid_e}, {"m": (lo_m, hi_m), "e": (lo_e, hi_e)}
    for g, (part, row) in enumerate(GROUP):

        def step(q, carry, g=g, part=part, row=row):
            o0 = q * WIDE
            pieces = [masked_piece(observed, tissue, g, o0 + i + 2) for i in range(WIDE)]
            done = z_pass(jnp.concatenate(pieces, axis=0), z_ref[0])
            for i in range(WIDE):
                put(mids[part], row, o0 + i, done[128 * i : 128 * i + 128])
            return carry

        lax.fori_loop(0, MID // 8 // WIDE, step, 0, unroll=True)
        pieces = [masked_piece(observed, tissue, g, o) for o in EDGE_OCTETS]
        done = z_pass(jnp.concatenate(pieces, axis=0), z_ref[0])
        for i in range(4):
            put(edges[part][i // 2], row, i % 2, done[128 * i : 128 * i + 128])
    fill_strips(mid_e, lo_e, hi_e, lo_m, hi_m, *strips)


EDGE_PART = arr(32, HALF, BZ)
MID_PART = arr(32, MID, BZ)
STRIPS = [arr(HALF, BY, BZ)] * 2 + [arr(BX, HALF, BZ)] * 2
TILE_ARR = arr(EDGE, EDGE, BZ)


def own_parts(octets):
    return [arr(octets, 8 * BX, 128, dtype=bf16)] * 2


def halo_parts(octets):
    return [pltpu.VMEM((octets, 8 * 2 * HALF, 128), bf16)] * 2


def blur(kind, tissue, gives, base, field, weights):
    lo_m, lo_e, mid_m, mid_e, hi_m, hi_e, xs_lo, xs_hi, ys_lo, ys_hi = field
    wx, wy, we, wz = weights
    count = count_out(kind)
    ym = shift(ys_hi, "owner", 1)
    yp = shift(ys_lo, "owner", -1)
    xm = shift(xs_hi, "slab", 1)
    xp = shift(xs_lo, "slab", -1)
    if kind == "final":
        base_lo_m, base_lo_e, base_mid_m, base_mid_e, base_hi_m, base_hi_e = base
        base_c, base_d = [base_lo_m, base_hi_m], [base_lo_e, base_hi_e]
    else:
        base_mid_m = base_mid_e = base
        base_c = base_d = [base]
    own = [lo_m, lo_e, mid_m, mid_e, hi_m, hi_e]
    *new_mid_m, high, low = call(
        kernel_a(kind), kind + "_a", [MID_PART] * count + own_parts(MID // 8), [],
        [tissue], [base_mid_m, *own, wx, wy, wz], 4.0,
    )
    cm = shift(jnp.concatenate([ym[BX - HALF :], yp[BX - HALF :]], axis=1), "slab", 1)
    cp = shift(jnp.concatenate([ym[:HALF], yp[:HALF]], axis=1), "slab", -1)
    new_mid_e = call(
        kernel_b(kind), kind + "_b", [MID_PART] * count, halo_parts(MID // 8),
        [tissue], [base_mid_e, xm, xp, high, low, wx, wy, wz], 3.0,
    )
    *new_m, edge_high, edge_low = call(
        kernel_c(kind), kind + "_c", [EDGE_PART] * (2 * count) + own_parts(4), [],
        [tissue], [*base_c, ym, yp, *own, wx, we, wz], 2.0,
    )
    late = [xm, xp, cm, cp, edge_high, edge_low]
    if kind == "final":
        scratch = [pltpu.VMEM((32, HALF, BZ), f32)] * 2 + halo_parts(4)
        scratch += [pltpu.VMEM((TILES, EDGE, EDGE, BZ), f32), pltpu.SMEM((TILES,), jnp.int32)]
        return call(
            kernel_last, "final_d", [TILE_ARR] * (NSEND + 1), scratch,
            [tissue, gives],
            [*base_d, *late, new_mid_m[0], new_mid_e[0], *new_m, wx, we, wz], 2.0,
        )
    *new_e, xs_lo, xs_hi, ys_lo, ys_hi = call(
        kernel_d(kind), kind + "_d", [EDGE_PART] * (2 * count) + STRIPS, halo_parts(4),
        [tissue], [*base_d, *late, new_mid_e[-1], *new_m[-2:], wx, we, wz], 2.0,
    )
    fields = [
        [
            new_m[2 * f], new_e[2 * f], new_mid_m[f], new_mid_e[f], new_m[2 * f + 1],
            new_e[2 * f + 1],
        ]
        for f in range(count)
    ]
    return fields[:-1] + [fields[-1] + [xs_lo, xs_hi, ys_lo, ys_hi]]


def store_kernel(first, count):
    def run(takes, *refs):
        arrived, out, sems = refs[:count], refs[-2], refs[-1]
        me = lax.axis_index("owner")

        def copy(c):
            slot = jnp.maximum(takes[me, first + c], 0)
            return pltpu.make_async_copy(arrived[c], out.at[slot], sems.at[c])

        for c in range(count):

            @pl.when(takes[me, first + c] >= 0)
            def _(c=c):
                copy(c).start()

        for c in range(count):

            @pl.when(takes[me, first + c] >= 0)
            def _(c=c):
                copy(c).wait()

    return run


def store_call(takes, first, arrived, packed=None):
    any_spec = pl.BlockSpec(memory_space=pl.ANY)
    count = len(arrived)
    arrays = list(arrived) + ([] if packed is None else [packed])
    return pl.pallas_call(
        store_kernel(first, count),
        out_shape=jax.ShapeDtypeStruct((CAP, EDGE, EDGE, BZ), f32),
        in_specs=[SM] + [any_spec] * len(arrays),
        out_specs=any_spec,
        scratch_shapes=[pltpu.SemaphoreType.DMA((count,))],
        input_output_aliases={} if packed is None else {len(arrays): 0},
        compiler_params=PARAMS,
        name="store",
    )(takes, *arrays)


def shift(values, axis, step):
    count = lax.axis_size(axis)
    return lax.ppermute(values, axis, [(i, (i + step) % count) for i in range(count)])


def body(observed, tissue, point_spread):
    weights = make_weights(point_spread)
    gives = jnp.asarray(GIVES, jnp.int32)
    takes = np.asarray(TAKES, np.int32)
    outs = [EDGE_PART] * 2 + [MID_PART] * 2 + [EDGE_PART] * 2 + STRIPS
    scratch = [pltpu.VMEM((1, 256, 256), bf16)]
    field = call(first_kernel, "first", outs, scratch, [point_spread, tissue], [observed], 2.0)
    base = observed
    for iteration in range(ITERS):
        (field,) = blur("ratio", tissue, gives, observed, field, weights)
        if iteration < ITERS - 1:
            base, field = blur("update", tissue, gives, base, field, weights)
    *sends, kept = blur("final", tissue, gives, base, field, weights)
    arrived = [
        lax.ppermute(send, "owner", [(e[0], e[1]) for e in step])
        for send, step in zip(sends, SENDS)
    ]
    last = NSEND - 2
    packed = store_call(takes[:, list(range(last)) + [NSEND]], 0, arrived[:last] + [kept])
    return store_call(takes[:, last:NSEND], 0, arrived[last:], packed)


def solution(mesh):
    in_specs = (P("slab", "owner", None), P("slab", "owner"), P())
    out_specs = P(("slab", "owner"), None, None, None)
    return jax.shard_map(body, mesh=mesh, in_specs=in_specs, out_specs=out_specs, check_vma=False)
```

```python
import jax
import jax.numpy as jnp
import numpy as np
from jax import lax
from jax.experimental import pallas as pl
from jax.experimental.pallas import tpu as pltpu
from jax.sharding import PartitionSpec as P

ITERS = 2
ratio_floor = 0.05

BX, BY, BZ = 64, 128, 128
TAPS, HALF = 33, 16
EDGE = 32
TILES = 8
CAP = 7
OWNERS = 16
MID = BY - 2 * HALF
WIDE = 12

bf16 = jnp.bfloat16
f32 = jnp.float32
VM = pl.BlockSpec(memory_space=pltpu.VMEM)
SM = pl.BlockSpec(memory_space=pltpu.SMEM)
PARAMS = pltpu.CompilerParams(vmem_limit_bytes=14 << 20)


GROUP = (("e", 0), ("m", 0), ("m", 16), ("e", 16))


def first_rank(c):
    return 7 * c if c % 2 == 0 else 7 * (c - 1) + 8


def tile_edges():
    out = []
    for c in range(OWNERS):
        for k in range(8 if c % 2 == 0 else 6):
            rank = first_rank(c) + k
            out.append((c, rank % OWNERS, k, rank // OWNERS))
    return out


ROUTES = (
    (6, 11, 0, 9, 2, 7, 12, 5, 14, 3, 8, 1, 10, 15, 4, 13),
    (2, 8, 1, 11, 15, 9, 0, 6, 10, 4, 13, 3, 5, 14, 7, 12),
    (7, 9, 4, 10, 14, 8, 13, 3, 11, 1, 12, 2, 6, 0, 5, -1),
    (3, 12, 5, 6, 13, -1, 11, 2, 15, 0, 7, 14, 9, 1, 8, 10),
    (4, -1, 14, -1, 1, 6, 15, -1, 12, 5, 9, -1, 8, -1, 3, 11),
    (5, 10, 15, 8, 3, 4, 1, -1, 13, 2, 11, 0, 7, 12, 9, 14),
    (-1, -1, -1, -1, 12, -1, 14, -1, -1, -1, -1, -1, 4, -1, 6, -1),
    (1, 13, 3, 7, 0, -1, 10, 4, 9, -1, 6, 15, 11, -1, 2, -1),
)
EDGES = tile_edges()
SENDS = [[e for e in EDGES if e[0] != e[1] and to[e[0]] == e[1]] for to in ROUTES]
NSEND = len(SENDS)
assert sum(map(len, SENDS)) + sum(e[0] == e[1] for e in EDGES) == len(EDGES)
GIVES = [[0] * (NSEND + 1) for _ in range(OWNERS)]
TAKES = [[-1] * (NSEND + 1) for _ in range(OWNERS)]
for _c, _step in enumerate(SENDS + [[e for e in EDGES if e[0] == e[1]]]):
    for _e in _step:
        GIVES[_e[0]][_c] = _e[2]
        TAKES[_e[1]][_c] = _e[3]


def parts(values):
    high = values.astype(bf16)
    return high, (values - high.astype(f32)).astype(bf16)


def band(taps_ref, axis, distance, flip):
    total = taps_ref[axis, 0]
    for k in range(1, TAPS):
        total = total + taps_ref[axis, k]
    acc = jnp.zeros(distance.shape, f32)
    for k in range(TAPS):
        tap = taps_ref[axis, TAPS - 1 - k if flip else k]
        acc = jnp.where(distance == k, tap, acc)
    return acc / total


def grid(rows, cols):
    return (
        lax.broadcasted_iota(jnp.int32, (rows, cols), 0),
        lax.broadcasted_iota(jnp.int32, (rows, cols), 1),
    )


def z_weights(taps_ref, flip, z_ref):
    r, c = grid(BZ, BZ)
    high, low = parts(band(taps_ref, 2, r - c + HALF, flip))
    z_ref[flip, 0:128, 0:128] = high
    z_ref[flip, 128:256, 0:128] = high
    z_ref[flip, 0:128, 128:256] = low
    z_ref[flip, 128:256, 128:256] = jnp.zeros((128, 128), bf16)


def weight_kernel(taps_ref, x_ref, y_ref, e_ref, z_ref):
    for flip in (0, 1):
        r, c = grid(128, 384)
        high, low = parts(band(taps_ref, 0, jnp.where((r % 8) == (c % 8), c // 8 - r // 8, -1), flip))
        x_ref[flip, :, 0:384] = high
        x_ref[flip, :, 384:768] = high
        x_ref[flip, :, 768:1152] = low
        r, c = grid(MID, BY)
        high, low = parts(band(taps_ref, 1, c - r, flip))
        y_ref[flip, :, 0:128] = high
        y_ref[flip, :, 128:256] = high
        y_ref[flip, :, 256:384] = low
        r, c = grid(64, 192)
        p = c - 48 * ((c >= 48).astype(jnp.int32) + (c >= 96) + (c >= 144))
        side = jnp.where(c >= 96, c - 96, c) >= 48
        same = ((r & 16) > 0) == side
        both = band(taps_ref, 1, jnp.where(same, p - (r & 15), -1), flip)
        high, low = parts(both)
        rest = jnp.where(c < 96, low.astype(f32), 0.0)
        e_ref[flip] = jnp.where(r < 32, high.astype(f32), rest).astype(bf16)
        z_weights(taps_ref, flip, z_ref)


def neighbours():
    row, me = lax.axis_index("slab"), lax.axis_index("owner")
    ends = [row > 0, row < lax.axis_size("slab") - 1, me > 0, me < lax.axis_size("owner") - 1]
    return [jnp.where(end, 1.0, 0.0).astype(f32) for end in ends]


def call(kernel, name, outs, scratch, small, arrays, micros=1.0):
    cost = pl.CostEstimate(
        flops=int(1.1e9 * micros), bytes_accessed=int(3.6e6 * micros), transcendentals=0
    )
    return pl.pallas_call(
        kernel,
        cost_estimate=cost,
        out_shape=tuple(outs),
        in_specs=[SM] * len(small) + [VM] * len(arrays),
        out_specs=(VM,) * len(outs),
        scratch_shapes=scratch,
        compiler_params=PARAMS,
        name=name,
    )(*small, *arrays)


def arr(*shape, dtype=f32):
    return jax.ShapeDtypeStruct(shape, dtype)


def make_weights(point_spread):
    outs = [
        arr(2, 128, 1152, dtype=bf16),
        arr(2, MID, 384, dtype=bf16),
        arr(2, 64, 192, dtype=bf16),
        arr(2, 256, 256, dtype=bf16),
    ]
    return call(weight_kernel, "weights", outs, [], [point_spread], [], 3.0)


def z_pass(rows, weights):
    high, low = parts(rows)
    both = jnp.dot(jnp.concatenate([high, low], axis=1), weights, preferred_element_type=f32)
    return both[:, :128] + both[:, 128:]


def keep(out, lines, row0, high_ref, low_ref):
    octets = out.shape[0] // 8
    out = jnp.concatenate(
        [out[:, 128 * i : 128 * i + 128].reshape(octets, 8, 128) for i in range(lines)], axis=1
    )
    high, low = parts(out)
    rows = pl.ds(pl.multiple_of(row0 * 8, 64), 8 * lines)
    high_ref[:, rows, :] = high
    low_ref[:, rows, :] = low


def y_mid(lines, weights, row0, high_ref, low_ref):
    high, low = parts(jnp.concatenate(lines, axis=1))
    out = jnp.dot(weights, jnp.concatenate([high, low, high], axis=0), preferred_element_type=f32)
    keep(out, len(lines), row0, high_ref, low_ref)


def y_edges(lines, weights, row0, high_ref, low_ref):
    high, low = parts(jnp.concatenate(lines, axis=1))
    out = jnp.dot(weights, jnp.concatenate([high, low], axis=0), preferred_element_type=f32)
    keep(out[:32] + out[32:], len(lines), row0, high_ref, low_ref)


def each_eight(rows, line, use):
    def step(i, carry):
        use([line(i * 8 + k) for k in range(8)], i * 8)
        return carry

    lax.fori_loop(0, rows // 8, step, 0, unroll=True)


def own_rows(make, use):
    each_eight(16, lambda r: make("e", r, r), lambda lines, r: use(lines, r))
    each_eight(32, lambda r: make("m", r, r + 16), lambda lines, r: use(lines, r + 16))
    each_eight(16, lambda r: make("e", r + 16, r + 48), lambda lines, r: use(lines, r + 48))


def x_dot(weights, high, low):
    return jnp.dot(
        weights, jnp.concatenate([high, low, high], axis=0), preferred_element_type=f32
    )


def split_lanes(out, count):
    return [out[:, 128 * i : 128 * i + 128] for i in range(count)]


def get(ref, row, octet):
    col = octet * 8 if isinstance(octet, int) else pl.multiple_of(octet * 8, 8)
    return ref[row : row + 16, pl.ds(col, 8), :].reshape(128, 128)


def put(ref, row, octet, piece):
    col = octet * 8 if isinstance(octet, int) else pl.multiple_of(octet * 8, 8)
    ref[row : row + 16, pl.ds(col, 8), :] = piece.reshape(16, 8, 128)


def masked_piece(observed, tissue, g, octet):
    return get(observed, 16 * g, octet) * tissue[g // 2, octet // 4].astype(f32)


def finish(kind, z_ref, pieces, bases):
    if kind == "ratio":
        return [[base / jnp.maximum(p, ratio_floor) for p, base in zip(pieces, bases)]]
    factor = z_pass(jnp.concatenate(pieces, axis=0), z_ref[1])
    new = jnp.concatenate(bases, axis=0) * factor
    fields = [new] if kind == "final" else [new, z_pass(new, z_ref[0])]
    return [
        [field[128 * i : 128 * i + 128] for i in range(len(pieces))] for field in fields
    ]


def count_out(kind):
    return 2 if kind == "update" else 1


def flip_of(kind):
    return 0 if kind == "ratio" else 1


def mid_finish(kind, tissue, base, z_ref, outs, g, o0, pieces):
    row = GROUP[g][1]
    bases = [
        get(base, row, o0 + i)
        if kind == "final"
        else masked_piece(base, tissue, g, o0 + i + 2)
        for i in range(WIDE)
    ]
    for ref, field in zip(outs, finish(kind, z_ref, pieces, bases)):
        for i in range(WIDE):
            put(ref, row, o0 + i, field[i])


EDGE_OCTETS = (0, 1, 14, 15)


def edge_finish(kind, tissue, base, z_ref, outs, groups, pieces):
    places = [(g, i) for g in groups for i in range(4)]
    bases = [
        get(base[i // 2], GROUP[g][1], i % 2)
        if kind == "final"
        else masked_piece(base[0], tissue, g, EDGE_OCTETS[i])
        for g, i in places
    ]
    for refs, field in zip(outs, finish(kind, z_ref, pieces, bases)):
        for (g, i), piece in zip(places, field):
            put(refs[i // 2], GROUP[g][1], i % 2, piece)


def kernel_a(kind):
    def run(tissue, base, lo_m, lo_e, mid_m, mid_e, hi_m, hi_e, x_ref, y_ref, z_ref, *outs):
        outs, (high_ref, low_ref) = outs[:-2], outs[-2:]
        flip = flip_of(kind)
        own = {"m": (lo_m, mid_m, hi_m), "e": (lo_e, mid_e, hi_e)}
        own_rows(
            lambda part, r, x: jnp.concatenate([ref[r] for ref in own[part]], axis=0),
            lambda lines, x: y_mid(lines, y_ref[flip], x, high_ref, low_ref),
        )

        def step(q, carry):
            o0 = q * WIDE
            for g in (1, 2):
                rows = slice(128 * (g - 1), 128 * (g - 1) + 384)
                high = jnp.concatenate([high_ref[o0 + i, rows] for i in range(WIDE)], axis=1)
                low = jnp.concatenate([low_ref[o0 + i, rows] for i in range(WIDE)], axis=1)
                pieces = split_lanes(x_dot(x_ref[flip], high, low), WIDE)
                mid_finish(kind, tissue, base, z_ref, outs, g, o0, pieces)
            return carry

        lax.fori_loop(0, MID // 8 // WIDE, step, 0, unroll=True)

    return run


def kernel_b(kind):
    def run(tissue, base, xm, xp, own_high, own_low, x_ref, y_ref, z_ref, *outs):
        outs, (high_ref, low_ref) = outs[:-2], outs[-2:]
        flip, inside = flip_of(kind), neighbours()
        for halo, near, row0 in ((xm, inside[0], 0), (xp, inside[1], 16)):
            each_eight(
                16,
                lambda r, halo=halo, near=near: halo[r] * near,
                lambda lines, r, row0=row0: y_mid(
                    lines, y_ref[flip], r + row0, high_ref, low_ref
                ),
            )

        def step(q, carry):
            o0 = q * WIDE
            for g in (0, 3):

                def rows(halo_ref, own_ref):
                    if g == 0:
                        both = [
                            jnp.concatenate(
                                [halo_ref[o0 + i, 0:128], own_ref[o0 + i, 0:256]], axis=0
                            )
                            for i in range(WIDE)
                        ]
                    else:
                        both = [
                            jnp.concatenate(
                                [own_ref[o0 + i, 256:512], halo_ref[o0 + i, 128:256]], axis=0
                            )
                            for i in range(WIDE)
                        ]
                    return jnp.concatenate(both, axis=1)

                out = x_dot(x_ref[flip], rows(high_ref, own_high), rows(low_ref, own_low))
                mid_finish(kind, tissue, base, z_ref, outs, g, o0, split_lanes(out, WIDE))
            return carry

        lax.fori_loop(0, MID // 8 // WIDE, step, 0, unroll=True)

    return run


def kernel_c(kind):
    def run(tissue, *refs):
        nbase = 2 if kind == "final" else 1
        base, refs = refs[:nbase], refs[nbase:]
        (ym, yp, lo_m, lo_e, mid_m, mid_e, hi_m, hi_e), refs = refs[:8], refs[8:]
        (x_ref, e_ref, z_ref), refs = refs[:3], refs[3:]
        outs, (high_ref, low_ref) = refs[:-2], refs[-2:]
        flip, inside = flip_of(kind), neighbours()
        own = {"m": (lo_m, mid_m, hi_m), "e": (lo_e, mid_e, hi_e)}

        def line(part, r, x):
            lo, mid, hi = own[part]
            return jnp.concatenate(
                [
                    ym[x] * inside[2],
                    lo[r],
                    mid[r, :HALF],
                    mid[r, MID - HALF :],
                    hi[r],
                    yp[x] * inside[3],
                ],
                axis=0,
            )

        own_rows(line, lambda lines, x: y_edges(lines, e_ref[flip], x, high_ref, low_ref))
        pieces = []
        for g in (1, 2):
            rows = slice(128 * (g - 1), 128 * (g - 1) + 384)
            high = jnp.concatenate([high_ref[i, rows] for i in range(4)], axis=1)
            low = jnp.concatenate([low_ref[i, rows] for i in range(4)], axis=1)
            pieces += split_lanes(x_dot(x_ref[flip], high, low), 4)
        pairs = [outs[2 * f : 2 * f + 2] for f in range(count_out(kind))]
        edge_finish(kind, tissue, base, z_ref, pairs, (1, 2), pieces)

    return run


def edge_d(kind, tissue, base, xm, xp, cm, cp, own_high, own_low, x_ref, e_ref, z_ref, pairs, high_ref, low_ref):
    flip, inside = flip_of(kind), neighbours()
    for halo, corner, near, row0 in ((xm, cm, inside[0], 0), (xp, cp, inside[1], 16)):

        def line(r, halo=halo, corner=corner, near=near):
            return jnp.concatenate(
                [
                    corner[r, :HALF] * (near * inside[2]),
                    halo[r, : 2 * HALF] * near,
                    halo[r, BY - 2 * HALF :] * near,
                    corner[r, HALF:] * (near * inside[3]),
                ],
                axis=0,
            )

        each_eight(
            16,
            line,
            lambda lines, r, row0=row0: y_edges(lines, e_ref[flip], r + row0, high_ref, low_ref),
        )
    pieces = []
    for g in (0, 3):

        def rows(halo_ref, own_ref):
            if g == 0:
                both = [
                    jnp.concatenate([halo_ref[i, 0:128], own_ref[i, 0:256]], axis=0)
                    for i in range(4)
                ]
            else:
                both = [
                    jnp.concatenate([own_ref[i, 256:512], halo_ref[i, 128:256]], axis=0)
                    for i in range(4)
                ]
            return jnp.concatenate(both, axis=1)

        out = x_dot(x_ref[flip], rows(high_ref, own_high), rows(low_ref, own_low))
        pieces += split_lanes(out, 4)
    edge_finish(kind, tissue, base, z_ref, pairs, (0, 3), pieces)


def fill_strips(mid_e, lo_e, hi_e, lo_m, hi_m, xs_lo, xs_hi, ys_lo, ys_hi):
    for ref, ends, middle in ((ys_lo, lo_e, lo_m), (ys_hi, hi_e, hi_m)):
        ref[:16] = ends[:16]
        ref[16:48] = middle[...]
        ref[48:] = ends[16:]
    for ref, row in ((xs_lo, 0), (xs_hi, 16)):
        ref[:, :HALF, :] = lo_e[row : row + 16]
        ref[:, HALF : BY - HALF, :] = mid_e[row : row + 16]
        ref[:, BY - HALF :, :] = hi_e[row : row + 16]


def kernel_d(kind):
    def run(tissue, base, xm, xp, cm, cp, own_high, own_low, mid_e, lo_m, hi_m, x_ref, e_ref, z_ref, *outs):
        outs, edges, (high_ref, low_ref) = outs[:-6], outs[-6:-2], outs[-2:]
        pairs = [outs[2 * f : 2 * f + 2] for f in range(count_out(kind))]
        edge_d(
            kind, tissue, (base,), xm, xp, cm, cp, own_high, own_low,
            x_ref, e_ref, z_ref, pairs, high_ref, low_ref,
        )
        fill_strips(mid_e, *pairs[-1], lo_m, hi_m, *edges)

    return run


def kernel_last(tissue, gives, base_lo, base_hi, xm, xp, cm, cp, own_high, own_low, mid_m, mid_e, lo_m, hi_m, x_ref, e_ref, z_ref, *refs):
    sends, (lo_e, hi_e, high_ref, low_ref, tiles, nth) = refs[: NSEND + 1], refs[NSEND + 1 :]
    for t in range(TILES):
        nth[t] = 0
    count = jnp.int32(0)
    for t in range(TILES):
        flag = tissue[t // 4, t % 4]

        @pl.when(flag > 0)
        def _(t=t, count=count):
            nth[count] = t

        count = count + (flag > 0).astype(jnp.int32)
    edge_d(
        "final", tissue, (base_lo, base_hi), xm, xp, cm, cp, own_high, own_low,
        x_ref, e_ref, z_ref, [(lo_e, hi_e)], high_ref, low_ref,
    )
    for i in range(2):
        for (lo, mid, hi), row, half in (
            ((lo_e, mid_e, hi_e), 16 * i, 16 * i),
            ((lo_m, mid_m, hi_m), 16 * i, 16 * (1 - i)),
        ):
            rows, into = slice(row, row + 16), slice(half, half + 16)
            tiles[4 * i, into, :HALF] = lo[rows]
            tiles[4 * i, into, HALF:] = mid[rows, :HALF]
            tiles[4 * i + 1, into] = mid[rows, HALF : HALF + EDGE]
            tiles[4 * i + 2, into] = mid[rows, HALF + EDGE : HALF + 2 * EDGE]
            tiles[4 * i + 3, into, :HALF] = mid[rows, MID - HALF :]
            tiles[4 * i + 3, into, HALF:] = hi[rows]
    for c, send in enumerate(sends):
        send[...] = tiles[nth[gives[lax.axis_index("owner"), c]]]


def first_kernel(taps_ref, tissue, observed, lo_m, lo_e, mid_m, mid_e, hi_m, hi_e, *strips):
    strips, z_ref = strips[:-1], strips[-1]
    z_weights(taps_ref, 0, z_ref)
    mids, edges = {"m": mid_m, "e": mid_e}, {"m": (lo_m, hi_m), "e": (lo_e, hi_e)}
    for g, (part, row) in enumerate(GROUP):

        def step(q, carry, g=g, part=part, row=row):
            o0 = q * WIDE
            pieces = [masked_piece(observed, tissue, g, o0 + i + 2) for i in range(WIDE)]
            done = z_pass(jnp.concatenate(pieces, axis=0), z_ref[0])
            for i in range(WIDE):
                put(mids[part], row, o0 + i, done[128 * i : 128 * i + 128])
            return carry

        lax.fori_loop(0, MID // 8 // WIDE, step, 0, unroll=True)
        pieces = [masked_piece(observed, tissue, g, o) for o in EDGE_OCTETS]
        done = z_pass(jnp.concatenate(pieces, axis=0), z_ref[0])
        for i in range(4):
            put(edges[part][i // 2], row, i % 2, done[128 * i : 128 * i + 128])
    fill_strips(mid_e, lo_e, hi_e, lo_m, hi_m, *strips)


EDGE_PART = arr(32, HALF, BZ)
MID_PART = arr(32, MID, BZ)
STRIPS = [arr(HALF, BY, BZ)] * 2 + [arr(BX, HALF, BZ)] * 2
TILE_ARR = arr(EDGE, EDGE, BZ)


def own_parts(octets):
    return [arr(octets, 8 * BX, 128, dtype=bf16)] * 2


def halo_parts(octets):
    return [pltpu.VMEM((octets, 8 * 2 * HALF, 128), bf16)] * 2


def blur(kind, tissue, gives, base, field, weights):
    lo_m, lo_e, mid_m, mid_e, hi_m, hi_e, xs_lo, xs_hi, ys_lo, ys_hi = field
    wx, wy, we, wz = weights
    count = count_out(kind)
    ym = shift(ys_hi, "owner", 1)
    yp = shift(ys_lo, "owner", -1)
    xm = shift(xs_hi, "slab", 1)
    xp = shift(xs_lo, "slab", -1)
    if kind == "final":
        base_lo_m, base_lo_e, base_mid_m, base_mid_e, base_hi_m, base_hi_e = base
        base_c, base_d = [base_lo_m, base_hi_m], [base_lo_e, base_hi_e]
    else:
        base_mid_m = base_mid_e = base
        base_c = base_d = [base]
    own = [lo_m, lo_e, mid_m, mid_e, hi_m, hi_e]
    *new_mid_m, high, low = call(
        kernel_a(kind), kind + "_a", [MID_PART] * count + own_parts(MID // 8), [],
        [tissue], [base_mid_m, *own, wx, wy, wz], 4.0,
    )
    cm = shift(jnp.concatenate([ym[BX - HALF :], yp[BX - HALF :]], axis=1), "slab", 1)
    cp = shift(jnp.concatenate([ym[:HALF], yp[:HALF]], axis=1), "slab", -1)
    new_mid_e = call(
        kernel_b(kind), kind + "_b", [MID_PART] * count, halo_parts(MID // 8),
        [tissue], [base_mid_e, xm, xp, high, low, wx, wy, wz], 3.0,
    )
    *new_m, edge_high, edge_low = call(
        kernel_c(kind), kind + "_c", [EDGE_PART] * (2 * count) + own_parts(4), [],
        [tissue], [*base_c, ym, yp, *own, wx, we, wz], 2.0,
    )
    late = [xm, xp, cm, cp, edge_high, edge_low]
    if kind == "final":
        scratch = [pltpu.VMEM((32, HALF, BZ), f32)] * 2 + halo_parts(4)
        scratch += [pltpu.VMEM((TILES, EDGE, EDGE, BZ), f32), pltpu.SMEM((TILES,), jnp.int32)]
        return call(
            kernel_last, "final_d", [TILE_ARR] * (NSEND + 1), scratch,
            [tissue, gives],
            [*base_d, *late, new_mid_m[0], new_mid_e[0], *new_m, wx, we, wz], 2.0,
        )
    *new_e, xs_lo, xs_hi, ys_lo, ys_hi = call(
        kernel_d(kind), kind + "_d", [EDGE_PART] * (2 * count) + STRIPS, halo_parts(4),
        [tissue], [*base_d, *late, new_mid_e[-1], *new_m[-2:], wx, we, wz], 2.0,
    )
    fields = [
        [
            new_m[2 * f], new_e[2 * f], new_mid_m[f], new_mid_e[f], new_m[2 * f + 1],
            new_e[2 * f + 1],
        ]
        for f in range(count)
    ]
    return fields[:-1] + [fields[-1] + [xs_lo, xs_hi, ys_lo, ys_hi]]


def store_kernel(first, count):
    def run(takes, *refs):
        arrived, out, sems = refs[:count], refs[-2], refs[-1]
        me = lax.axis_index("owner")

        def copy(c):
            slot = jnp.maximum(takes[me, first + c], 0)
            return pltpu.make_async_copy(arrived[c], out.at[slot], sems.at[c])

        for c in range(count):

            @pl.when(takes[me, first + c] >= 0)
            def _(c=c):
                copy(c).start()

        for c in range(count):

            @pl.when(takes[me, first + c] >= 0)
            def _(c=c):
                copy(c).wait()

    return run


def store_call(takes, first, arrived, packed=None):
    any_spec = pl.BlockSpec(memory_space=pl.ANY)
    count = len(arrived)
    arrays = list(arrived) + ([] if packed is None else [packed])
    return pl.pallas_call(
        store_kernel(first, count),
        out_shape=jax.ShapeDtypeStruct((CAP, EDGE, EDGE, BZ), f32),
        in_specs=[SM] + [any_spec] * len(arrays),
        out_specs=any_spec,
        scratch_shapes=[pltpu.SemaphoreType.DMA((count,))],
        input_output_aliases={} if packed is None else {len(arrays): 0},
        compiler_params=PARAMS,
        name="store",
    )(takes, *arrays)


def shift(values, axis, step):
    count = lax.axis_size(axis)
    return lax.ppermute(values, axis, [(i, (i + step) % count) for i in range(count)])


def body(observed, tissue, point_spread):
    weights = make_weights(point_spread)
    gives = jnp.asarray(GIVES, jnp.int32)
    takes = np.asarray(TAKES, np.int32)
    outs = [EDGE_PART] * 2 + [MID_PART] * 2 + [EDGE_PART] * 2 + STRIPS
    scratch = [pltpu.VMEM((1, 256, 256), bf16)]
    field = call(first_kernel, "first", outs, scratch, [point_spread, tissue], [observed], 2.0)
    base = observed
    for iteration in range(ITERS):
        (field,) = blur("ratio", tissue, gives, observed, field, weights)
        if iteration < ITERS - 1:
            base, field = blur("update", tissue, gives, base, field, weights)
    *sends, kept = blur("final", tissue, gives, base, field, weights)
    arrived = [
        lax.ppermute(send, "owner", [(e[0], e[1]) for e in step])
        for send, step in zip(sends, SENDS)
    ]
    last = NSEND - 2
    packed = store_call(takes[:, list(range(last)) + [NSEND]], 0, arrived[:last] + [kept])
    return store_call(takes[:, last:NSEND], 0, arrived[last:], packed)


def solution(mesh):
    in_specs = (P("slab", "owner", None), P("slab", "owner"), P())
    out_specs = P(("slab", "owner"), None, None, None)
    return jax.shard_map(body, mesh=mesh, in_specs=in_specs, out_specs=out_specs, check_vma=False)
```
